512 devices in a mesh: outer: 32 (over x, y, z_hi), inner: 16 (over z_lo, core).
Axes of the slice: x: 4, y: 4, z: 16 (z_hi: 2, z_lo: 8; z = z_hi * 8 + z_lo), core: 2. Of those that a mesh axis runs over, the one named last changes fastest.
Arguments:
- notes: bfloat16 [20480, 512], P('outer'), may hold values from -8 to 8
- timelines: bfloat16 [20480, 512], P(('outer', 'inner')), may hold values from -8 to 8
- partner: int32 [20480], P('outer'), may hold values from 0 to 20479, each once
- note_days: int32 [20480], P('outer'), may hold values from 0 to 479
- time_days: int32 [20480], P(('outer', 'inner')), may hold values from 0 to 479
- logit_scale: float32 [1], replicated, may hold values from 0.25 to 0.5
- bias: float32 [8], replicated, may hold values from -2 to 2
Outputs:
- mean_loss: float32 [1], replicated
- bias_grad: float32 [8], replicated
- note_grad: float32 [20480, 512], P(('outer', 'inner'))
- time_grad: float32 [20480, 512], P(('outer', 'inner'))
The draws below stay inside these ranges and needn't reach their ends.
Inputs may be any that keep to these rules, and one draw needn't show every extreme that they name: Each timeline is the partner of exactly one note.
All inputs are finite; a program needn't handle non-finite values.
Results may differ from the reference program's by a relative error of at most 0.00255.
Values may be sent and summed in bfloat16 or wider, within the bound.
A program may use at most 64 MiB of HBM per device.

```python
import math
import jax
import jax.numpy as jnp
from jax import lax

D = 512
NB = 8
PAIRS = 20480


def row_spread(key, lower, upper):
    return jnp.exp(jax.random.uniform(key, (PAIRS,), jnp.float32, math.log(lower), math.log(upper)))


def finish(values, spread):
    ramp = 1.0 + 2.0 * jnp.arange(PAIRS, dtype=jnp.float32) / max(PAIRS - 1, 1)
    return jnp.clip(values * spread[:, None] * ramp[:, None], -8.0, 8.0)


def draw_notes(key, part):
    key = jax.random.fold_in(key, 11)
    first_key, second_key = jax.random.split(key)
    values = jax.random.normal(first_key, (PAIRS, D), jnp.float32)
    values = finish(values, row_spread(second_key, 0.2, 2.0))
    return values.astype(jnp.bfloat16)


def draw_timelines(key, part):
    key = jax.random.fold_in(key, 23)
    first_key, second_key = jax.random.split(key)
    values = jax.random.normal(first_key, (PAIRS, D), jnp.float32)
    values = finish(values, row_spread(second_key, 0.2, 2.0))
    return values.astype(jnp.bfloat16)


def plant(drawn, stream_key, smallest, largest):
    longest = drawn.shape.index(max(drawn.shape))
    spots = []
    for shift in (0, 1):
        where = [jax.random.randint(jax.random.fold_in(stream_key, axis), (), 0, length) for axis, length in enumerate(drawn.shape)]
        where[longest] = (where[longest] + shift) % drawn.shape[longest]
        spots.append(tuple(where))
    return drawn.at[spots[0]].set(smallest).at[spots[1]].set(largest)


def setup_inputs(seed: int = 0) -> dict:
    keys = jax.random.split(jax.random.key(seed), 8)
    notes = draw_notes(jax.random.fold_in(keys[7], 71), 0)
    timelines = draw_timelines(jax.random.fold_in(keys[7], 71), 0)
    partner = jax.random.permutation(keys[2], PAIRS).astype(jnp.int32)
    note_days = plant(jax.random.randint(keys[3], (PAIRS,), 0, 480), jax.random.fold_in(keys[3], 1), 0, 479).astype(jnp.int32)
    time_days = plant(jax.random.randint(keys[4], (PAIRS,), 0, 480), jax.random.fold_in(keys[4], 1), 0, 479).astype(jnp.int32)
    logit_scale = jnp.clip(jax.random.uniform(keys[5], (1,), jnp.float32, 0.25, 0.5), 0.25, 0.5)
    bias = jnp.clip(jax.random.uniform(keys[6], (NB,), jnp.float32, -2.0, 2.0), -2.0, 2.0)
    return dict(notes=notes, timelines=timelines, partner=partner, note_days=note_days, time_days=time_days, logit_scale=logit_scale, bias=bias)


bucket_days = 30

def pair_logits(note_rows, note_when, timelines, time_days, scale, bias):
    raw = jnp.dot(note_rows, timelines.T, preferred_element_type=jnp.float32)
    bucket = jnp.minimum(jnp.abs(note_when[:, None] - time_days[None, :]) // bucket_days, bias.shape[0] - 1).astype(jnp.int32)
    return (raw * scale + jnp.take(bias, bucket), bucket)

def combine_stats(first, second):
    peak = jnp.maximum(first[0], second[0])
    return (peak, first[1] * jnp.exp(first[0] - peak) + second[1] * jnp.exp(second[0] - peak))

def reference(notes, timelines, partner, note_days, time_days, logit_scale, bias):
    pairs = notes.shape[0]
    block = math.gcd(pairs, 512)
    blocks = pairs // block
    scale = logit_scale[0] / math.sqrt(D)
    time_index = jnp.arange(pairs, dtype=jnp.int32)
    inputs = (notes.reshape(blocks, block, D), partner.reshape(blocks, block), note_days.reshape(blocks, block))

    def first_pass(carry, item):
        note_rows, mates, when = item
        logits, bucket = pair_logits(note_rows, when, timelines, time_days, scale, bias)
        peak = lax.optimization_barrier(jnp.max(logits, axis=1))
        row_logsum = peak + jnp.log(lax.optimization_barrier(jnp.sum(jnp.exp(logits - peak[:, None]), axis=1)))
        col_peak = lax.optimization_barrier(jnp.max(logits, axis=0))
        col_total = lax.optimization_barrier(jnp.sum(jnp.exp(logits - col_peak[None, :]), axis=0))
        merged = combine_stats((carry[0], carry[1]), (col_peak, col_total))
        positive = jnp.sum(jnp.where(mates[:, None] == time_index[None, :], logits, 0.0))
        return ((merged[0], merged[1], carry[2] + positive), row_logsum)
    start = (jnp.full((pairs,), -1e+30, jnp.float32), jnp.zeros((pairs,), jnp.float32), jnp.zeros((), jnp.float32))
    (col_peak, col_total, pos_total), row_logsum = lax.scan(first_pass, start, inputs)
    col_logsum = col_peak + jnp.log(col_total)
    row_flat = row_logsum.reshape(pairs)

    def second_pass(carry, item):
        note_rows, mates, when, row_part = item
        logits, bucket = pair_logits(note_rows, when, timelines, time_days, scale, bias)
        positive = (mates[:, None] == time_index[None, :]).astype(jnp.float32)
        dlogit = 0.5 * jnp.exp(logits - row_part[:, None]) + 0.5 * jnp.exp(logits - col_logsum[None, :]) - positive
        weights = dlogit.astype(jnp.bfloat16)
        note_part = scale * jnp.dot(weights, timelines, preferred_element_type=jnp.float32)
        time_acc = carry[0] + jnp.dot(weights.T, note_rows, preferred_element_type=jnp.float32)
        bucket_acc = carry[1] + jnp.stack([jnp.sum(jnp.where(bucket == level, dlogit, 0.0)) for level in range(bias.shape[0])])
        return ((time_acc, bucket_acc), note_part)
    start_two = (jnp.zeros((pairs, D), jnp.float32), jnp.zeros((bias.shape[0],), jnp.float32))
    (time_acc, bucket_acc), note_parts = lax.scan(second_pass, start_two, inputs + (row_logsum,))
    mean_loss = (0.5 * jnp.sum(row_flat) + 0.5 * jnp.sum(col_logsum) - pos_total) / pairs
    return (mean_loss.reshape(1), bucket_acc / pairs, note_parts.reshape(pairs, D), scale * time_acc)
```

```python
import functools
import math

import jax
import jax.numpy as jnp
from jax import lax
from jax.experimental import pallas as pl
from jax.experimental.pallas import tpu as pltpu
from jax.sharding import PartitionSpec as P

BUCKET_DAYS = 30
LOG2E = math.log2(math.e)
LN2 = math.log(2.0)
MESH = pl.DeviceIdType.MESH
F32 = jnp.float32
BF16 = jnp.bfloat16


def log2_sum(parts):
    peak = functools.reduce(jnp.maximum, parts)
    total = functools.reduce(jnp.add, [jnp.exp2(part - peak) for part in parts])
    return peak + jnp.log2(total)


def spread_rows(row, width):
    return jnp.broadcast_to(row, (width, row.shape[1])).T


def kernel(
    sizes,
    scale_ref, bias_ref, notes_ref, time_ref, when_ref, note_when_ref, partner_ref,
    note_grad_ref, time_grad_ref, summary_ref,
    shards, shard_days, stage, planes, logits, weights, when_col, partner_col, row_col, spare,
    row_stats, col_stats, col_far, part, time_out, time_in, far_in,
    note_near, note_out, note_in, note_own, level_sums, inner_sums, plane_sums, far_sums,
    g_send, g_recv, d_send, d_recv, r_send, r_recv, c_send, c_recv, t_send, t_recv,
    n_send, n_recv, m_send, m_recv, a_send, a_recv, b_send, b_recv,
):
    nx, ny, nz = sizes
    nq = nx * ny
    rows, depth = notes_ref.shape
    own = time_ref.shape[0]
    span = nq * own
    step = min(128, rows)
    blocks = rows // step
    wide = when_col.shape[1]
    levels = bias_ref.shape[0]

    outer_id, inner_id = lax.axis_index("outer"), lax.axis_index("inner")
    q, far = outer_id // 2, outer_id % 2
    qx, qy = q // ny, q % ny
    line, core = inner_id // 2, inner_id % 2

    def plane_peer(s):
        return lax.rem(qx + s // ny, nx) * ny + lax.rem(qy + s % ny, ny)

    def in_plane(peer):
        return (peer * 2 + far, inner_id)

    across = (q * 2 + 1 - far, inner_id)

    def inner_peer(s):
        return lax.rem(inner_id + s, 2 * nz)

    def send(src, dst, send_sem, recv_sem, device):
        pltpu.make_async_remote_copy(
            src_ref=src, dst_ref=dst, send_sem=send_sem, recv_sem=recv_sem,
            device_id=device, device_id_type=MESH,
        ).start()

    def wait_in(dst, recv_sem):
        pltpu.make_async_copy(dst, dst, recv_sem).wait()

    wait_out = wait_in

    barrier = pltpu.get_barrier_semaphore()

    def hello_plane(s, _):
        pl.semaphore_signal(barrier, inc=1, device_id=in_plane(plane_peer(s)), device_id_type=MESH)
        return 0

    def hello_inner(s, _):
        pl.semaphore_signal(barrier, inc=1, device_id=(outer_id, inner_peer(s)), device_id_type=MESH)
        return 0

    pl.semaphore_signal(barrier, inc=1, device_id=across, device_id_type=MESH)
    lax.fori_loop(1, nq, hello_plane, 0)
    lax.fori_loop(1, 2 * nz, hello_inner, 0)

    scale = scale_ref[0] * F32(LOG2E / math.sqrt(depth))
    lane = lax.broadcasted_iota(jnp.int32, (1, span), 1)
    lane_q = ((lane.astype(F32) + 0.5) * F32(1.0 / own)).astype(jnp.int32)
    shards[0, q] = time_ref[...]
    shard_days[0, q] = jnp.where(lane_q == q, when_ref[...].astype(F32), 0.0)
    pl.semaphore_wait(barrier, 1 + (nq - 1) + (2 * nz - 1))

    send(time_ref, shards.at[1, q], g_send.at[1, q], g_recv.at[1, q], across)
    send(shard_days.at[0, q], shard_days.at[1, q], d_send.at[1, q], d_recv.at[1, q], across)

    def share(plane):
        def one(s, _):
            peer = plane_peer(s)
            send(shards.at[plane, q], shards.at[plane, q], g_send.at[plane, peer], g_recv.at[plane, q], in_plane(peer))
            send(shard_days.at[plane, q], shard_days.at[plane, q], d_send.at[plane, peer], d_recv.at[plane, q],
                 in_plane(peer))
            return 0
        lax.fori_loop(1, nq, one, 0)

    share(0)
    when_col[...] = spread_rows(note_when_ref[...].astype(F32), wide)
    partner_col[...] = spread_rows(partner_ref[...].astype(F32), wide)
    wait_in(shards.at[1, q], g_recv.at[1, q])
    wait_in(shard_days.at[1, q], d_recv.at[1, q])
    share(1)

    def gap(block, plane, days):
        return jnp.abs(when_col[pl.ds(block * step, step), 0:1] - days)

    def ids(plane):
        zone = far if plane == 0 else 1 - far
        return (((lane_q * 2 + zone) * (2 * nz) + inner_id) * own + (lane - lane_q * own)).astype(F32)

    def plane_days(plane):
        return functools.reduce(jnp.add, [shard_days[plane, k] for k in range(nq)])

    positive = jnp.zeros((8, span), F32)
    col_logs = []
    for plane in range(2):
        def arrive(s, _):
            peer = plane_peer(s)
            wait_in(shards.at[plane, peer], g_recv.at[plane, peer])
            wait_in(shard_days.at[plane, peer], d_recv.at[plane, peer])
            return 0
        lax.fori_loop(1, nq, arrive, 0)

        def settle(k, _):
            stage[pl.ds(pl.multiple_of(k * own, own), own)] = shards[plane, k].astype(F32)
            return 0
        lax.fori_loop(0, nq, settle, 0)
        planes[plane] = stage[...].astype(BF16)
        days = plane_days(plane)
        names = ids(plane)
        cols = pl.ds(plane * span, span)

        def logit_block(block, carry):
            col_peak, positive = carry
            here = pl.ds(pl.multiple_of(block * step, step), step)
            raw = lax.dot_general(notes_ref[here], planes[plane], (((1,), (1,)), ((), ())),
                                  preferred_element_type=F32)
            distance = gap(block, plane, days)
            offset = jnp.full(raw.shape, bias_ref[0] * F32(LOG2E), F32)
            for level in range(1, levels):
                offset = jnp.where(distance >= F32(BUCKET_DAYS * level), bias_ref[level] * F32(LOG2E), offset)
            value = raw * scale + offset
            logits[here, cols] = value
            peak = jnp.max(value, axis=1, keepdims=True)
            total = jnp.sum(jnp.exp2(value - peak), axis=1, keepdims=True)
            spare[plane, here] = jnp.broadcast_to(peak + jnp.log2(total), (step, wide))
            hit = jnp.where(partner_col[here, 0:1] == names, value, 0.0)
            positive = positive + jnp.sum(hit.reshape(step // 8, 8, span), axis=0)
            return (jnp.maximum(col_peak, jnp.max(value, axis=0, keepdims=True)), positive)

        col_peak, positive = lax.fori_loop(
            0, blocks, logit_block, (jnp.full((1, span), -jnp.inf, F32), positive))

        def col_block(block, total):
            here = pl.ds(pl.multiple_of(block * step, step), step)
            return total + jnp.sum(jnp.exp2(logits[here, cols] - col_peak), axis=0, keepdims=True)

        col_total = lax.fori_loop(0, blocks, col_block, jnp.zeros((1, span), F32))
        col_logs.append(col_peak + jnp.log2(col_total))

    row_stats[inner_id] = log2_sum([spare[0], spare[1]]).T[0:1]

    def share_rows(s, _):
        peer = inner_peer(s)
        send(row_stats.at[inner_id], row_stats.at[inner_id], r_send.at[peer], r_recv.at[inner_id], (outer_id, peer))
        return 0

    for plane in range(2):
        col_stats[q, 0:1, pl.ds(plane * span, span)] = col_logs[plane]

    def share_cols(s, _):
        peer = plane_peer(s)
        send(col_stats.at[q], col_stats.at[q], c_send.at[peer], c_recv.at[q], in_plane(peer))
        return 0

    lax.fori_loop(1, nq, share_cols, 0)
    lax.fori_loop(1, 2 * nz, share_rows, 0)

    def cols_in(s, _):
        peer = plane_peer(s)
        wait_in(col_stats.at[peer], c_recv.at[peer])
        return 0

    lax.fori_loop(1, nq, cols_in, 0)
    near = log2_sum([col_stats[k] for k in range(nq)])
    col_far[0] = near
    send(col_far.at[0], col_far.at[1], c_send.at[q], c_recv.at[q], across)

    def rows_in(s, _):
        peer = inner_peer(s)
        wait_in(row_stats.at[peer], r_recv.at[peer])
        return 0

    lax.fori_loop(1, 2 * nz, rows_in, 0)
    row_log = log2_sum([row_stats[k] for k in range(2 * nz)])
    row_col[...] = spread_rows(row_log + 1.0, wide)
    wait_in(col_far.at[1], c_recv.at[q])
    there = col_far[1]
    col_log = [
        log2_sum([near[:, :span], there[:, span:]]),
        log2_sum([near[:, span:], there[:, :span]]),
    ]

    for plane in (1, 0):
        cols = pl.ds(plane * span, span)
        names = ids(plane)
        col_half = col_log[plane] + 1.0

        def weight_block(block, _):
            here = pl.ds(pl.multiple_of(block * step, step), step)
            value = logits[here, cols]
            value = (
                jnp.exp2(value - row_col[here, 0:1])
                + jnp.exp2(value - col_half)
                - jnp.where(partner_col[here, 0:1] == names, 1.0, 0.0)
            )
            logits[here, cols] = value
            weights[here, cols] = value.astype(BF16)
            return 0

        lax.fori_loop(0, blocks, weight_block, 0)

        wide_step = min(128, span)

        def time_block(block, _):
            here = pl.ds(pl.multiple_of(block * wide_step, wide_step), wide_step)
            from_here = pl.ds(pl.multiple_of(plane * span + block * wide_step, wide_step), wide_step)
            stage[here] = lax.dot_general(weights[:, from_here], notes_ref[...], (((0,), (0,)), ((), ())),
                                          preferred_element_type=F32)
            return 0

        lax.fori_loop(0, span // wide_step, time_block, 0)

        def share_time(s, _):
            peer = plane_peer(s)
            time_out[plane, peer] = stage[pl.ds(pl.multiple_of(peer * own, own), own)].astype(BF16)
            send(time_out.at[plane, peer], time_in.at[plane, q], t_send.at[plane, peer], t_recv.at[plane, q],
                 in_plane(peer))
            return 0

        lax.fori_loop(1, nq, share_time, 0)
        part[plane] = stage[pl.ds(pl.multiple_of(q * own, own), own)]

    def note_block(block, _):
        here = pl.ds(pl.multiple_of(block * step, step), step)
        stage_rows = jnp.dot(weights[here, 0:span], planes[0], preferred_element_type=F32)
        note_own[here] = stage_rows + jnp.dot(weights[here, span:2 * span], planes[1], preferred_element_type=F32)
        return 0

    lax.fori_loop(0, blocks, note_block, 0)

    def share_core(k, _):
        there = pl.ds(pl.multiple_of((2 * k + 1 - core) * own, own), own)
        send(note_own.at[there], note_near.at[k], n_send.at[k], n_recv.at[k], (outer_id, 2 * line + 1 - core))
        return 0

    lax.fori_loop(0, nz, share_core, 0)

    level_sums[...] = jnp.zeros_like(level_sums)
    for plane in range(2):
        days = plane_days(plane)
        cols = pl.ds(plane * span, span)

        def level_block(block, _):
            here = pl.ds(pl.multiple_of(block * step, step), step)
            value = logits[here, cols]
            distance = gap(block, plane, days)
            for level in range(levels):
                picked = value if level == 0 else jnp.where(distance >= F32(BUCKET_DAYS * level), value, 0.0)
                level_sums[level] += jnp.sum(picked.reshape(step // 8, 8, span), axis=0)
            return 0

        if plane == 0:
            lax.fori_loop(0, blocks, level_block, 0)

            def share_line(s, _):
                k = lax.rem(line + s, nz)
                wait_in(note_near.at[k], n_recv.at[k])
                mine = pl.ds(pl.multiple_of((2 * k + core) * own, own), own)
                note_out[k] = (note_own[mine] + note_near[k]).astype(BF16)
                send(note_out.at[k], note_in.at[line], m_send.at[k], m_recv.at[line], (outer_id, 2 * k + core))
                return 0

            lax.fori_loop(1, nz, share_line, 0)
        else:
            lax.fori_loop(0, blocks, level_block, 0)

    above = jnp.sum(jnp.sum(level_sums[...], axis=1), axis=1, keepdims=True)
    below = jnp.concatenate([above[1:], jnp.zeros((1, 1), F32)], axis=0)
    loss = F32(LN2) * (
        (0.5 / (2 * nz)) * jnp.sum(row_log)
        + (0.5 / (2 * nq)) * (jnp.sum(col_log[0]) + jnp.sum(col_log[1]))
        - jnp.sum(positive)
    )
    column = lax.broadcasted_iota(jnp.int32, (levels, wide), 1)
    inner_sums[inner_id] = jnp.where(column == 0, above - below, jnp.where(column == 1, loss, 0.0))

    def share_sums(s, _):
        peer = inner_peer(s)
        send(inner_sums.at[inner_id], inner_sums.at[inner_id], a_send.at[peer], a_recv.at[inner_id], (outer_id, peer))
        return 0

    lax.fori_loop(1, 2 * nz, share_sums, 0)

    def time_arrive(plane):
        def one(s, _):
            peer = plane_peer(s)
            wait_in(time_in.at[plane, peer], t_recv.at[plane, peer])
            part[plane] += time_in[plane, peer].astype(F32)
            return 0
        lax.fori_loop(1, nq, one, 0)

    time_arrive(1)
    send(part.at[1], far_in, t_send.at[1, q], t_recv.at[1, q], across)

    def sums_in(s, _):
        peer = inner_peer(s)
        wait_in(inner_sums.at[peer], a_recv.at[peer])
        return 0

    lax.fori_loop(1, 2 * nz, sums_in, 0)
    plane_sums[q] = functools.reduce(jnp.add, [inner_sums[k] for k in range(2 * nz)])

    def share_plane_sums(s, _):
        peer = plane_peer(s)
        send(plane_sums.at[q], plane_sums.at[q], b_send.at[peer], b_recv.at[q], in_plane(peer))
        return 0

    lax.fori_loop(1, nq, share_plane_sums, 0)
    time_arrive(0)

    def plane_sums_in(s, _):
        peer = plane_peer(s)
        wait_in(plane_sums.at[peer], b_recv.at[peer])
        return 0

    lax.fori_loop(1, nq, plane_sums_in, 0)
    far_sums[0] = functools.reduce(jnp.add, [plane_sums[k] for k in range(nq)])
    send(far_sums.at[0], far_sums.at[1], b_send.at[q], b_recv.at[q], across)

    factor = scale_ref[0] * F32(1.0 / math.sqrt(depth))
    wait_in(note_near.at[line], n_recv.at[line])
    total = note_own[pl.ds(pl.multiple_of((2 * line + core) * own, own), own)] + note_near[line]
    spare_total = total

    def note_arrive(s, total):
        k = lax.rem(line + s, nz)
        wait_in(note_in.at[k], m_recv.at[k])
        return total + note_in[k].astype(F32)

    note_grad_ref[...] = factor * lax.fori_loop(1, nz, note_arrive, spare_total)
    wait_in(far_in, t_recv.at[1, q])
    time_grad_ref[...] = factor * (part[0] + far_in[...])
    wait_in(far_sums.at[1], b_recv.at[q])
    summary_ref[...] = (far_sums[0] + far_sums[1]) * F32(1.0 / (rows * 2 * nq))

    wait_out(time_ref, g_send.at[1, q])
    wait_out(shard_days.at[0, q], d_send.at[1, q])
    wait_out(col_far.at[0], c_send.at[q])
    wait_out(part.at[1], t_send.at[1, q])
    wait_out(far_sums.at[0], b_send.at[q])

    def plane_left(s, _):
        peer = plane_peer(s)
        for plane in range(2):
            wait_out(shards.at[plane, q], g_send.at[plane, peer])
            wait_out(shard_days.at[plane, q], d_send.at[plane, peer])
            wait_out(time_out.at[plane, peer], t_send.at[plane, peer])
        wait_out(col_stats.at[q], c_send.at[peer])
        wait_out(plane_sums.at[q], b_send.at[peer])
        return 0

    def inner_left(s, _):
        peer = inner_peer(s)
        wait_out(row_stats.at[inner_id], r_send.at[peer])
        wait_out(inner_sums.at[inner_id], a_send.at[peer])
        return 0

    def core_left(k, _):
        there = pl.ds(pl.multiple_of((2 * k + 1 - core) * own, own), own)
        wait_out(note_own.at[there], n_send.at[k])
        return 0

    def line_left(s, _):
        k = lax.rem(line + s, nz)
        wait_out(note_out.at[k], m_send.at[k])
        return 0

    lax.fori_loop(1, nq, plane_left, 0)
    lax.fori_loop(1, 2 * nz, inner_left, 0)
    lax.fori_loop(0, nz, core_left, 0)
    lax.fori_loop(1, nz, line_left, 0)


def body(notes, timelines, partner, note_days, time_days, logit_scale, bias):
    rows, depth = notes.shape
    own = timelines.shape[0]
    nq = lax.axis_size("outer") // 2
    nz = lax.axis_size("inner") // 2
    ny = 2 ** (int(math.log2(nq)) // 2)
    span = nq * own
    levels = bias.shape[0]
    wide = 128
    vmem, smem = pl.BlockSpec(memory_space=pltpu.VMEM), pl.BlockSpec(memory_space=pltpu.SMEM)
    dma = pltpu.SemaphoreType.DMA
    note_grad, time_grad, summary = pl.pallas_call(
        functools.partial(kernel, (nq // ny, ny, nz)),
        out_shape=(
            jax.ShapeDtypeStruct((own, depth), F32),
            jax.ShapeDtypeStruct((own, depth), F32),
            jax.ShapeDtypeStruct((levels, wide), F32),
        ),
        in_specs=[smem, smem] + [vmem] * 5,
        out_specs=(vmem,) * 3,
        scratch_shapes=[
            pltpu.VMEM((2, nq, own, depth), BF16),
            pltpu.VMEM((2, nq, 1, span), F32),
            pltpu.VMEM((span, depth), F32),
            pltpu.VMEM((2, span, depth), BF16),
            pltpu.VMEM((rows, 2 * span), F32),
            pltpu.VMEM((rows, 2 * span), BF16),
            pltpu.VMEM((rows, wide), F32),
            pltpu.VMEM((rows, wide), F32),
            pltpu.VMEM((rows, wide), F32),
            pltpu.VMEM((2, rows, wide), F32),
            pltpu.VMEM((2 * nz, 1, rows), F32),
            pltpu.VMEM((nq, 1, 2 * span), F32),
            pltpu.VMEM((2, 1, 2 * span), F32),
            pltpu.VMEM((2, own, depth), F32),
            pltpu.VMEM((2, nq, own, depth), BF16),
            pltpu.VMEM((2, nq, own, depth), BF16),
            pltpu.VMEM((own, depth), F32),
            pltpu.VMEM((nz, own, depth), F32),
            pltpu.VMEM((nz, own, depth), BF16),
            pltpu.VMEM((nz, own, depth), BF16),
            pltpu.VMEM((rows, depth), F32),
            pltpu.VMEM((levels, 8, span), F32),
            pltpu.VMEM((2 * nz, levels, wide), F32),
            pltpu.VMEM((nq, levels, wide), F32),
            pltpu.VMEM((2, levels, wide), F32),
            dma((2, nq)), dma((2, nq)), dma((2, nq)), dma((2, nq)),
            dma((2 * nz,)), dma((2 * nz,)), dma((nq,)), dma((nq,)),
            dma((2, nq)), dma((2, nq)),
            dma((nz,)), dma((nz,)), dma((nz,)), dma((nz,)),
            dma((2 * nz,)), dma((2 * nz,)), dma((nq,)), dma((nq,)),
        ],
        compiler_params=pltpu.CompilerParams(
            collective_id=0, has_side_effects=True, vmem_limit_bytes=48 * 2**20
        ),
    )(
        logit_scale, bias, notes, timelines,
        jnp.tile(time_days, nq).reshape(1, span),
        note_days.reshape(1, rows),
        partner.reshape(1, rows),
    )
    return (summary[0, 1:2], summary[:, 0], note_grad, time_grad)


def solution(mesh):
    placed = (
        P("outer", None),
        P(("outer", "inner"), None),
        P("outer"),
        P("outer"),
        P(("outer", "inner")),
        P(),
        P(),
    )
    return jax.shard_map(
        body,
        mesh=mesh,
        in_specs=placed,
        out_specs=(P(), P(), P(("outer", "inner"), None), P(("outer", "inner"), None)),
        check_vma=False,
    )
```

```python
import functools
import math

import jax
import jax.numpy as jnp
from jax import lax
from jax.experimental import pallas as pl
from jax.experimental.pallas import tpu as pltpu
from jax.sharding import PartitionSpec as P

BUCKET_DAYS = 30
LOG2E = math.log2(math.e)
LN2 = math.log(2.0)
MESH = pl.DeviceIdType.MESH
F32 = jnp.float32
BF16 = jnp.bfloat16


def log2_sum(parts):
    peak = functools.reduce(jnp.maximum, parts)
    total = functools.reduce(jnp.add, [jnp.exp2(part - peak) for part in parts])
    return peak + jnp.log2(total)


def spread_rows(row, width):
    return jnp.broadcast_to(row, (width, row.shape[1])).T


def kernel(
    sizes,
    scale_any, bias_any, notes_any, time_any, when_any, note_when_any, partner_any,
    note_grad_ref, time_grad_ref, summary_ref,
    scale_ref, bias_ref, notes_ref, note_when_ref, partner_ref,
    shards, shard_days, stage, planes, logits, raws, weights, when_col, partner_col, row_col, spare,
    row_stats, col_stats, col_far, part, time_out, time_in, far_out, far_in,
    note_near, note_out, note_in, note_own, level_sums, ring_sums, plane_sums,
    l_sem, g_send, g_recv, d_send, d_recv, r_send, r_recv, c_send, c_recv, f_send, f_recv, t_send, t_recv,
    n_send, n_recv, m_send, m_recv, a_send, a_recv, b_send, b_recv,
):
    nx, ny, nz = sizes
    nq, group = nx * ny, 2 * nz
    rows, depth = notes_ref.shape
    own = time_any.shape[0]
    span = nq * own
    step = min(128, rows)
    blocks = rows // step
    wide = when_col.shape[1]
    levels = bias_ref.shape[0]

    outer_id, inner_id = lax.axis_index("outer"), lax.axis_index("inner")
    q, far = outer_id // 2, outer_id % 2
    qx, qy = q // ny, q % ny
    line, core = inner_id // 2, inner_id % 2
    ring_id = far * group + inner_id

    def plane_peer(s):
        return lax.rem(qx + s // ny, nx) * ny + lax.rem(qy + s % ny, ny)

    def in_plane(peer):
        return (peer * 2 + far, inner_id)

    across = (q * 2 + 1 - far, inner_id)

    def inner_peer(s):
        return lax.rem(inner_id + s, group)

    def ring_peer(s):
        return lax.rem(ring_id + s, 2 * group)

    def on_ring(peer):
        return (q * 2 + peer // group, peer % group)

    def send(src, dst, send_sem, recv_sem, device):
        pltpu.make_async_remote_copy(
            src_ref=src, dst_ref=dst, send_sem=send_sem, recv_sem=recv_sem,
            device_id=device, device_id_type=MESH,
        ).start()

    def wait_in(dst, recv_sem):
        pltpu.make_async_copy(dst, dst, recv_sem).wait()

    wait_out = wait_in

    def each(count, one):
        def run(s, _):
            one(s)
            return 0
        lax.fori_loop(1, count, run, 0)

    barrier = pltpu.get_barrier_semaphore()

    def hello(device):
        pl.semaphore_signal(barrier, inc=1, device_id=device, device_id_type=MESH)

    each(nq, lambda s: hello(in_plane(plane_peer(s))))
    each(2 * group, lambda s: hello(on_ring(ring_peer(s))))

    loads = [
        pltpu.make_async_copy(src, dst, l_sem.at[k])
        for k, (src, dst) in enumerate((
            (time_any, shards.at[0, q]), (when_any, shard_days.at[0, q]), (scale_any, scale_ref), (bias_any, bias_ref),
            (note_when_any, note_when_ref), (partner_any, partner_ref), (notes_any, notes_ref),
        ))
    ]
    for load in loads:
        load.start()
    for load in loads:
        load.wait()
    pl.semaphore_wait(barrier, (nq - 1) + (2 * group - 1))

    send(shards.at[0, q], shards.at[1, q], g_send.at[1, q], g_recv.at[1, q], across)
    send(shard_days.at[0, q], shard_days.at[1, q], d_send.at[1, q], d_recv.at[1, q], across)

    def share(plane):
        def one(s):
            peer = plane_peer(s)
            send(shard_days.at[plane, q], shard_days.at[plane, q], d_send.at[plane, peer], d_recv.at[plane, q],
                 in_plane(peer))
            send(shards.at[plane, q], shards.at[plane, q], g_send.at[plane, peer], g_recv.at[plane, q], in_plane(peer))
        each(nq, one)

    share(0)
    scale = scale_ref[...] * F32(LOG2E / math.sqrt(depth))
    lane = lax.broadcasted_iota(jnp.int32, (1, span), 1)
    lane_q = ((lane.astype(F32) + 0.5) * F32(1.0 / own)).astype(jnp.int32)
    lane_r = lane - lane_q * own
    when_col[...] = spread_rows(note_when_ref[...].reshape(1, rows).astype(F32), wide)
    partner_col[...] = spread_rows(partner_ref[...].reshape(1, rows).astype(F32), wide)
    place = jnp.where(lax.broadcasted_iota(jnp.int32, (own, span), 0) == lane_r, 1.0, 0.0).astype(BF16)

    def plane_days(plane):
        days = jnp.concatenate([shard_days[plane, k] for k in range(nq)], axis=0).astype(F32)
        high = jnp.floor(days * F32(1.0 / 16.0))
        low = days - high * 16.0
        placed = 16.0 * jnp.dot(high.astype(BF16), place, preferred_element_type=F32) + jnp.dot(
            low.astype(BF16), place, preferred_element_type=F32)
        mine = lax.broadcasted_iota(jnp.int32, (nq, span), 0) == lane_q
        return jnp.sum(jnp.where(mine, placed, 0.0), axis=0, keepdims=True)

    def gap(here, days):
        return jnp.abs(when_col[here, 0:1] - days)

    def ids(plane):
        zone = far if plane == 0 else 1 - far
        return (((lane_q * 2 + zone) * group + inner_id) * own + lane_r).astype(F32)

    def by_rows(one, start):
        def run(block, carry):
            return one(pl.ds(pl.multiple_of(block * step, step), step), carry)
        return lax.fori_loop(0, blocks, run, start)

    def cols_of(plane):
        return pl.ds(plane * span, span)

    def days_in(plane):
        def one(s):
            peer = plane_peer(s)
            wait_in(shard_days.at[plane, peer], d_recv.at[plane, peer])
        each(nq, one)
        days = plane_days(plane)

        def offset_block(here, _):
            distance = gap(here, days)
            offset = jnp.full((step, span), bias_ref[0] * F32(LOG2E), F32)
            for level in range(1, levels):
                offset = jnp.where(distance >= F32(BUCKET_DAYS * level), bias_ref[level] * F32(LOG2E), offset)
            logits[here, cols_of(plane)] = offset
            return 0

        by_rows(offset_block, 0)
        return days

    def plane_in(plane):
        def one(s):
            peer = plane_peer(s)
            wait_in(shards.at[plane, peer], g_recv.at[plane, peer])
        each(nq, one)

        def settle(k, _):
            stage[pl.ds(pl.multiple_of(k * own, own), own)] = shards[plane, k].astype(F32)
            return 0
        lax.fori_loop(0, nq, settle, 0)
        planes[plane] = stage[...].astype(BF16)
        cols = cols_of(plane)

        raws[...] = lax.dot_general(notes_ref[...], planes[plane], (((1,), (1,)), ((), ())),
                                    preferred_element_type=F32)

        def logit_block(here, col_peak):
            value = raws[here] * scale + logits[here, cols]
            logits[here, cols] = value
            peak = jnp.max(value, axis=1, keepdims=True)
            total = jnp.sum(jnp.exp2(value - peak), axis=1, keepdims=True)
            spare[plane, here] = jnp.broadcast_to(peak + jnp.log2(total), (step, wide))
            return jnp.maximum(col_peak, jnp.max(value, axis=0, keepdims=True))

        col_peak = by_rows(logit_block, jnp.full((1, span), -jnp.inf, F32))

        def col_block(here, total):
            return total + jnp.sum(jnp.exp2(logits[here, cols] - col_peak), axis=0, keepdims=True)

        col_stats[plane, q] = col_peak + jnp.log2(by_rows(col_block, jnp.zeros((1, span), F32)))

        def share_cols(s):
            peer = plane_peer(s)
            send(col_stats.at[plane, q], col_stats.at[plane, q], c_send.at[plane, peer], c_recv.at[plane, q],
                 in_plane(peer))
        each(nq, share_cols)

    def cols_in(plane):
        def one(s):
            peer = plane_peer(s)
            wait_in(col_stats.at[plane, peer], c_recv.at[plane, peer])
        each(nq, one)
        near = log2_sum([col_stats[plane, k] for k in range(nq)])
        col_far[plane] = near
        send(col_far.at[plane], col_far.at[2 + 1 - plane], f_send.at[plane], f_recv.at[1 - plane], across)
        return near

    def cols_done(plane, near):
        wait_in(col_far.at[2 + plane], f_recv.at[plane])
        return log2_sum([near, col_far[2 + plane]])

    near_days = days_in(0)
    wait_in(shards.at[1, q], g_recv.at[1, q])
    wait_in(shard_days.at[1, q], d_recv.at[1, q])
    share(1)
    plane_in(0)
    far_days = days_in(1)
    near_cols = cols_in(0)
    plane_in(1)

    row_stats[inner_id] = log2_sum([spare[0], spare[1]]).T[0:1]

    def share_rows(s):
        peer = inner_peer(s)
        send(row_stats.at[inner_id], row_stats.at[inner_id], r_send.at[peer], r_recv.at[inner_id], (outer_id, peer))

    each(group, share_rows)
    far_cols = cols_in(1)

    def rows_in(s):
        peer = inner_peer(s)
        wait_in(row_stats.at[peer], r_recv.at[peer])

    each(group, rows_in)
    row_log = log2_sum([row_stats[k] for k in range(group)])
    row_col[...] = spread_rows(row_log + 1.0, wide)
    level_sums[...] = jnp.zeros_like(level_sums)

    def weigh(plane, col_log, positive):
        cols = cols_of(plane)
        names = ids(plane)
        col_half = col_log + 1.0

        def weight_block(here, positive):
            value = logits[here, cols]
            hit = partner_col[here, 0:1] == names
            slope = (
                jnp.exp2(value - row_col[here, 0:1]) + jnp.exp2(value - col_half) - jnp.where(hit, 1.0, 0.0)
            )
            logits[here, cols] = slope
            weights[here, cols] = slope.astype(BF16)
            return positive + jnp.sum(jnp.where(hit, value, 0.0).reshape(step // 8, 8, span), axis=0)

        return by_rows(weight_block, positive)

    def time_partials(plane):
        stage[...] = lax.dot_general(weights[:, plane * span:(plane + 1) * span], notes_ref[...],
                                     (((0,), (0,)), ((), ())), preferred_element_type=F32)

        def share_time(s):
            peer = plane_peer(s)
            time_out[plane, peer] = stage[pl.ds(pl.multiple_of(peer * own, own), own)].astype(BF16)
            send(time_out.at[plane, peer], time_in.at[plane, q], t_send.at[plane, peer], t_recv.at[plane, q],
                 in_plane(peer))

        each(nq, share_time)
        part[plane] = stage[pl.ds(pl.multiple_of(q * own, own), own)]

    def add_levels(plane, days):
        cols = cols_of(plane)

        def level_block(here, _):
            value = logits[here, cols]
            distance = gap(here, days)
            for level in range(levels):
                picked = value if level == 0 else jnp.where(distance >= F32(BUCKET_DAYS * level), value, 0.0)
                level_sums[level] += jnp.sum(picked.reshape(step // 8, 8, span), axis=0)
            return 0

        by_rows(level_block, 0)

    far_log = cols_done(1, far_cols)
    positive = weigh(1, far_log, jnp.zeros((8, span), F32))
    time_partials(1)
    note_own[...] = jnp.dot(weights[:, span:2 * span], planes[1], preferred_element_type=F32)
    add_levels(1, far_days)
    near_log = cols_done(0, near_cols)
    positive = weigh(0, near_log, positive)

    note_own[...] += jnp.dot(weights[:, 0:span], planes[0], preferred_element_type=F32)

    def chunk(k, which):
        return pl.ds(pl.multiple_of((2 * k + which) * own, own), own)

    def share_core(s):
        k = lax.rem(line + s, nz)
        send(note_own.at[chunk(k, 1 - core)], note_near.at[k], n_send.at[k], n_recv.at[k],
             (outer_id, 2 * line + 1 - core))

    each(nz + 1, share_core)
    add_levels(0, near_days)

    above = jnp.sum(level_sums[...], axis=1)
    below = jnp.concatenate([above[1:], jnp.zeros((1, span), F32)], axis=0)
    loss = F32(LN2) * (
        (0.5 / group) * jnp.sum(row_log)
        + (0.5 / (2 * nq)) * (jnp.sum(near_log) + jnp.sum(far_log))
        - jnp.sum(positive)
    )
    buckets = jnp.sum(above - below, axis=1, keepdims=True)
    across_lanes = jnp.where(
        lax.broadcasted_iota(jnp.int32, (levels, wide), 0) == lax.broadcasted_iota(jnp.int32, (levels, wide), 1),
        buckets, 0.0)
    at_loss = lax.broadcasted_iota(jnp.int32, (1, wide), 1) == levels
    ring_sums[ring_id] = jnp.sum(across_lanes, axis=0, keepdims=True) + jnp.where(at_loss, loss, 0.0)

    def share_sums(s):
        peer = ring_peer(s)
        send(ring_sums.at[ring_id], ring_sums.at[ring_id], a_send.at[peer], a_recv.at[ring_id], on_ring(peer))

    each(2 * group, share_sums)

    def share_line(s):
        k = lax.rem(line + s, nz)
        wait_in(note_near.at[k], n_recv.at[k])
        note_out[k] = (note_own[chunk(k, core)] + note_near[k]).astype(BF16)
        send(note_out.at[k], note_in.at[line], m_send.at[k], m_recv.at[line], (outer_id, 2 * k + core))

    each(nz, share_line)
    time_partials(0)

    def time_arrive(plane):
        def one(s):
            peer = plane_peer(s)
            wait_in(time_in.at[plane, peer], t_recv.at[plane, peer])
            part[plane] += time_in[plane, peer].astype(F32)
        each(nq, one)

    time_arrive(1)
    far_out[...] = part[1].astype(BF16)
    send(far_out, far_in, t_send.at[1, q], t_recv.at[1, q], across)

    def sums_in(s):
        peer = ring_peer(s)
        wait_in(ring_sums.at[peer], a_recv.at[peer])

    each(2 * group, sums_in)
    plane_sums[q] = functools.reduce(jnp.add, [ring_sums[k] for k in range(2 * group)])

    def share_plane_sums(s):
        peer = plane_peer(s)
        send(plane_sums.at[q], plane_sums.at[q], b_send.at[peer], b_recv.at[q], in_plane(peer))

    each(nq, share_plane_sums)
    time_arrive(0)

    factor = scale_ref[...] * F32(1.0 / math.sqrt(depth))
    wait_in(note_near.at[line], n_recv.at[line])
    note_near[line] += note_own[chunk(line, core)]

    def note_arrive(s):
        k = lax.rem(line + s, nz)
        wait_in(note_in.at[k], m_recv.at[k])
        note_near[line] += note_in[k].astype(F32)

    each(nz, note_arrive)
    note_grad_ref[...] = factor * note_near[line]

    def plane_sums_in(s):
        peer = plane_peer(s)
        wait_in(plane_sums.at[peer], b_recv.at[peer])

    each(nq, plane_sums_in)
    summary_ref[...] = functools.reduce(jnp.add, [plane_sums[k] for k in range(nq)]) * F32(1.0 / (rows * 2 * nq))
    wait_in(far_in, t_recv.at[1, q])
    time_grad_ref[...] = factor * (part[0] + far_in[...].astype(F32))

    wait_out(shards.at[0, q], g_send.at[1, q])
    wait_out(shard_days.at[0, q], d_send.at[1, q])
    wait_out(far_out, t_send.at[1, q])

    def plane_left(s):
        peer = plane_peer(s)
        for plane in range(2):
            wait_out(shards.at[plane, q], g_send.at[plane, peer])
            wait_out(shard_days.at[plane, q], d_send.at[plane, peer])
            wait_out(col_stats.at[plane, q], c_send.at[plane, peer])
            wait_out(time_out.at[plane, peer], t_send.at[plane, peer])
        wait_out(plane_sums.at[q], b_send.at[peer])

    def line_left(s):
        k = lax.rem(line + s, nz)
        wait_out(note_out.at[k], m_send.at[k])

    for plane in range(2):
        wait_out(col_far.at[plane], f_send.at[plane])
    each(nq, plane_left)
    each(group, lambda s: wait_out(row_stats.at[inner_id], r_send.at[inner_peer(s)]))
    each(2 * group, lambda s: wait_out(ring_sums.at[ring_id], a_send.at[ring_peer(s)]))
    each(nz + 1, lambda s: wait_out(note_near.at[0], n_send.at[lax.rem(line + s, nz)]))
    each(nz, line_left)


def hand_over(note_ref, time_ref, summary_ref, loss_ref, bias_ref, note_out, time_out):
    levels = bias_ref.shape[0]
    note_out[...] = note_ref[...]
    time_out[...] = time_ref[...]
    bias_ref[...] = summary_ref[0, 0:levels]
    loss_ref[...] = summary_ref[0, levels:levels + 1]


def body(notes, timelines, partner, note_days, time_days, logit_scale, bias):
    rows, depth = notes.shape
    own = timelines.shape[0]
    nq = lax.axis_size("outer") // 2
    nz = lax.axis_size("inner") // 2
    ny = 2 ** (int(math.log2(nq)) // 2)
    span = nq * own
    group = 2 * nz
    levels = bias.shape[0]
    wide = 128
    vmem, anywhere = pl.BlockSpec(memory_space=pltpu.VMEM), pl.BlockSpec(memory_space=pltpu.HBM)
    dma = pltpu.SemaphoreType.DMA
    grads = jax.ShapeDtypeStruct((own, depth), F32)
    note_grad, time_grad, summary = pl.pallas_call(
        functools.partial(kernel, (nq // ny, ny, nz)),
        out_shape=(grads, grads, jax.ShapeDtypeStruct((1, wide), F32)),
        in_specs=[anywhere] * 7,
        out_specs=(vmem,) * 3,
        scratch_shapes=[
            pltpu.VMEM((1, 1), F32),
            pltpu.SMEM((levels,), F32),
            pltpu.VMEM((rows, depth), BF16),
            pltpu.VMEM((rows,), jnp.int32),
            pltpu.VMEM((rows,), jnp.int32),
            pltpu.VMEM((2, nq, own, depth), BF16),
            pltpu.VMEM((2, nq, 1, own), jnp.int32),
            pltpu.VMEM((span, depth), F32),
            pltpu.VMEM((2, span, depth), BF16),
            pltpu.VMEM((rows, 2 * span), F32),
            pltpu.VMEM((rows, span), F32),
            pltpu.VMEM((rows, 2 * span), BF16),
            pltpu.VMEM((rows, wide), F32),
            pltpu.VMEM((rows, wide), F32),
            pltpu.VMEM((rows, wide), F32),
            pltpu.VMEM((2, rows, wide), F32),
            pltpu.VMEM((group, 1, rows), F32),
            pltpu.VMEM((2, nq, 1, span), F32),
            pltpu.VMEM((4, 1, span), F32),
            pltpu.VMEM((2, own, depth), F32),
            pltpu.VMEM((2, nq, own, depth), BF16),
            pltpu.VMEM((2, nq, own, depth), BF16),
            pltpu.VMEM((own, depth), BF16),
            pltpu.VMEM((own, depth), BF16),
            pltpu.VMEM((nz, own, depth), F32),
            pltpu.VMEM((nz, own, depth), BF16),
            pltpu.VMEM((nz, own, depth), BF16),
            pltpu.VMEM((rows, depth), F32),
            pltpu.VMEM((levels, 8, span), F32),
            pltpu.VMEM((2 * group, 1, wide), F32),
            pltpu.VMEM((nq, 1, wide), F32),
            dma((7,)),
            dma((2, nq)), dma((2, nq)), dma((2, nq)), dma((2, nq)),
            dma((group,)), dma((group,)), dma((2, nq)), dma((2, nq)), dma((2,)), dma((2,)),
            dma((2, nq)), dma((2, nq)),
            dma((nz,)), dma((nz,)), dma((nz,)), dma((nz,)),
            dma((2 * group,)), dma((2 * group,)), dma((nq,)), dma((nq,)),
        ],
        compiler_params=pltpu.CompilerParams(
            collective_id=0, has_side_effects=True, vmem_limit_bytes=56 * 2**20
        ),
    )(
        logit_scale.reshape(1, 1), bias, notes, timelines,
        time_days.reshape(1, own), note_days, partner,
    )
    mean_loss, bias_grad, note_grad, time_grad = pl.pallas_call(
        hand_over,
        out_shape=(jax.ShapeDtypeStruct((1,), F32), jax.ShapeDtypeStruct((levels,), F32), grads, grads),
        in_specs=[vmem] * 3,
        out_specs=(vmem,) * 4,
    )(note_grad, time_grad, summary)
    return (mean_loss, bias_grad, note_grad, time_grad)


def solution(mesh):
    placed = (
        P("outer", None),
        P(("outer", "inner"), None),
        P("outer"),
        P("outer"),
        P(("outer", "inner")),
        P(),
        P(),
    )
    return jax.shard_map(
        body,
        mesh=mesh,
        in_specs=placed,
        out_specs=(P(), P(), P(("outer", "inner"), None), P(("outer", "inner"), None)),
        check_vma=False,
    )
```

```python
import functools
import math

import jax
import jax.numpy as jnp
from jax import lax
from jax.experimental import pallas as pl
from jax.experimental.pallas import tpu as pltpu
from jax.sharding import PartitionSpec as P

BUCKET_DAYS = 30
LOG2E = math.log2(math.e)
LN2 = math.log(2.0)
MESH = pl.DeviceIdType.MESH
F32 = jnp.float32
BF16 = jnp.bfloat16


def log2_sum(parts):
    peak = functools.reduce(jnp.maximum, parts)
    total = functools.reduce(jnp.add, [jnp.exp2(part - peak) for part in parts])
    return peak + jnp.log2(total)


def spread_rows(row, width):
    return jnp.broadcast_to(row, (width, row.shape[1])).T


def kernel(
    sizes,
    scale_any, bias_any, notes_any, time_any, when_any, note_when_any, partner_any,
    note_grad_ref, time_grad_ref, summary_ref,
    scale_ref, bias_ref, notes_ref, note_when_ref, partner_ref,
    shards, shard_days, stage, planes, logits, raws, weights, when_col, partner_col, row_col, spare,
    row_stats, col_stats, col_far, part, time_out, time_in, far_out, far_in,
    note_near, note_out, note_in, pair_out, pair_in, note_own, level_sums, ring_sums, plane_sums,
    l_sem, g_send, g_recv, d_send, d_recv, r_send, r_recv, c_send, c_recv, f_send, f_recv, t_send, t_recv,
    n_send, n_recv, m_send, m_recv, p_send, p_recv, a_send, a_recv, b_send, b_recv,
):
    nx, ny, nz = sizes
    nq, group = nx * ny, 2 * nz
    rows, depth = notes_ref.shape
    own = time_any.shape[0]
    span = nq * own
    step = min(128, rows)
    blocks = rows // step
    wide = when_col.shape[1]
    levels = bias_ref.shape[0]

    outer_id, inner_id = lax.axis_index("outer"), lax.axis_index("inner")
    q, far = outer_id // 2, outer_id % 2
    qx, qy = q // ny, q % ny
    line, core = inner_id // 2, inner_id % 2
    ring_id = far * group + inner_id

    def plane_peer(s):
        return lax.rem(qx + s // ny, nx) * ny + lax.rem(qy + s % ny, ny)

    def in_plane(peer):
        return (peer * 2 + far, inner_id)

    across = (q * 2 + 1 - far, inner_id)

    def inner_peer(s):
        return lax.rem(inner_id + s, group)

    def ring_peer(s):
        return lax.rem(ring_id + s, 2 * group)

    def on_ring(peer):
        return (q * 2 + peer // group, peer % group)

    def send(src, dst, send_sem, recv_sem, device):
        pltpu.make_async_remote_copy(
            src_ref=src, dst_ref=dst, send_sem=send_sem, recv_sem=recv_sem,
            device_id=device, device_id_type=MESH,
        ).start()

    def wait_in(dst, recv_sem):
        pltpu.make_async_copy(dst, dst, recv_sem).wait()

    wait_out = wait_in

    def each(count, one):
        def run(s, _):
            one(s)
            return 0
        lax.fori_loop(1, count, run, 0)

    barrier = pltpu.get_barrier_semaphore()

    def hello(device):
        pl.semaphore_signal(barrier, inc=1, device_id=device, device_id_type=MESH)

    def hello_far(s, _):
        hello((q * 2 + 1 - far, inner_peer(s)))
        return 0

    lax.fori_loop(0, group, hello_far, 0)
    each(group, lambda s: hello((outer_id, inner_peer(s))))
    each(nq, lambda s: hello(in_plane(plane_peer(s))))

    loads = [
        pltpu.make_async_copy(src, dst, l_sem.at[k])
        for k, (src, dst) in enumerate((
            (time_any, shards.at[0, q]), (when_any, shard_days.at[0, q]), (scale_any, scale_ref), (bias_any, bias_ref),
            (note_when_any, note_when_ref), (partner_any, partner_ref), (notes_any, notes_ref),
        ))
    ]
    for load in loads:
        load.start()
    for load in loads:
        load.wait()
    pl.semaphore_wait(barrier, (nq - 1) + (2 * group - 1))

    send(shards.at[0, q], shards.at[1, q], g_send.at[1, q], g_recv.at[1, q], across)
    send(shard_days.at[0, q], shard_days.at[1, q], d_send.at[1, q], d_recv.at[1, q], across)

    def share(plane):
        def one(s):
            peer = plane_peer(s)
            send(shard_days.at[plane, q], shard_days.at[plane, q], d_send.at[plane, peer], d_recv.at[plane, q],
                 in_plane(peer))
            send(shards.at[plane, q], shards.at[plane, q], g_send.at[plane, peer], g_recv.at[plane, q], in_plane(peer))
        each(nq, one)

    share(0)
    scale = scale_ref[...] * F32(LOG2E / math.sqrt(depth))
    lane = lax.broadcasted_iota(jnp.int32, (1, span), 1)
    lane_q = ((lane.astype(F32) + 0.5) * F32(1.0 / own)).astype(jnp.int32)
    lane_r = lane - lane_q * own
    when_col[...] = spread_rows(note_when_ref[...].reshape(1, rows).astype(F32), wide)
    partner_col[...] = spread_rows(partner_ref[...].reshape(1, rows).astype(F32), wide)
    place = jnp.where(lax.broadcasted_iota(jnp.int32, (own, span), 0) == lane_r, 1.0, 0.0).astype(BF16)

    def plane_days(plane):
        days = jnp.concatenate([shard_days[plane, k] for k in range(nq)], axis=0).astype(F32)
        high = jnp.floor(days * F32(1.0 / 16.0))
        low = days - high * 16.0
        placed = 16.0 * jnp.dot(high.astype(BF16), place, preferred_element_type=F32) + jnp.dot(
            low.astype(BF16), place, preferred_element_type=F32)
        mine = lax.broadcasted_iota(jnp.int32, (nq, span), 0) == lane_q
        return jnp.sum(jnp.where(mine, placed, 0.0), axis=0, keepdims=True)

    def gap(here, days):
        return jnp.abs(when_col[here, 0:1] - days)

    def ids(plane):
        zone = far if plane == 0 else 1 - far
        return (((lane_q * 2 + zone) * group + inner_id) * own + lane_r).astype(F32)

    def by_rows(one, start):
        def run(block, carry):
            return one(pl.ds(pl.multiple_of(block * step, step), step), carry)
        return lax.fori_loop(0, blocks, run, start)

    def cols_of(plane):
        return pl.ds(plane * span, span)

    def days_in(plane):
        def one(s):
            peer = plane_peer(s)
            wait_in(shard_days.at[plane, peer], d_recv.at[plane, peer])
        each(nq, one)
        days = plane_days(plane)

        def offset_block(here, _):
            distance = gap(here, days)
            offset = jnp.full((step, span), bias_ref[0] * F32(LOG2E), F32)
            for level in range(1, levels):
                offset = jnp.where(distance >= F32(BUCKET_DAYS * level), bias_ref[level] * F32(LOG2E), offset)
            logits[here, cols_of(plane)] = offset
            return 0

        by_rows(offset_block, 0)
        return days

    def plane_in(plane):
        def one(s):
            peer = plane_peer(s)
            wait_in(shards.at[plane, peer], g_recv.at[plane, peer])
        each(nq, one)

        def settle(k, _):
            stage[pl.ds(pl.multiple_of(k * own, own), own)] = shards[plane, k].astype(F32)
            return 0
        lax.fori_loop(0, nq, settle, 0)
        planes[plane] = stage[...].astype(BF16)
        cols = cols_of(plane)

        raws[...] = lax.dot_general(notes_ref[...], planes[plane], (((1,), (1,)), ((), ())),
                                    preferred_element_type=F32)

        def logit_block(here, col_peak):
            value = raws[here] * scale + logits[here, cols]
            logits[here, cols] = value
            peak = jnp.max(value, axis=1, keepdims=True)
            total = jnp.sum(jnp.exp2(value - peak), axis=1, keepdims=True)
            spare[plane, here] = jnp.broadcast_to(peak + jnp.log2(total), (step, wide))
            return jnp.maximum(col_peak, jnp.max(value, axis=0, keepdims=True))

        col_peak = by_rows(logit_block, jnp.full((1, span), -jnp.inf, F32))

        def col_block(here, total):
            return total + jnp.sum(jnp.exp2(logits[here, cols] - col_peak), axis=0, keepdims=True)

        col_stats[plane, q] = col_peak + jnp.log2(by_rows(col_block, jnp.zeros((1, span), F32)))

        def share_cols(s):
            peer = plane_peer(s)
            send(col_stats.at[plane, q], col_stats.at[plane, q], c_send.at[plane, peer], c_recv.at[plane, q],
                 in_plane(peer))
        each(nq, share_cols)

    def cols_in(plane):
        def one(s):
            peer = plane_peer(s)
            wait_in(col_stats.at[plane, peer], c_recv.at[plane, peer])
        each(nq, one)
        near = log2_sum([col_stats[plane, k] for k in range(nq)])
        col_far[plane] = near
        send(col_far.at[plane], col_far.at[2 + 1 - plane], f_send.at[plane], f_recv.at[1 - plane], across)
        return near

    def cols_done(plane, near):
        wait_in(col_far.at[2 + plane], f_recv.at[plane])
        return log2_sum([near, col_far[2 + plane]])

    near_days = days_in(0)
    wait_in(shards.at[1, q], g_recv.at[1, q])
    wait_in(shard_days.at[1, q], d_recv.at[1, q])
    share(1)
    plane_in(0)
    far_days = days_in(1)
    near_cols = cols_in(0)
    plane_in(1)

    row_stats[inner_id] = log2_sum([spare[0], spare[1]]).T[0:1]

    def share_rows(s):
        peer = inner_peer(s)
        send(row_stats.at[inner_id], row_stats.at[inner_id], r_send.at[peer], r_recv.at[inner_id], (outer_id, peer))

    each(group, share_rows)
    far_cols = cols_in(1)

    def rows_in(s):
        peer = inner_peer(s)
        wait_in(row_stats.at[peer], r_recv.at[peer])

    each(group, rows_in)
    row_log = log2_sum([row_stats[k] for k in range(group)])
    row_col[...] = spread_rows(row_log + 1.0, wide)
    level_sums[...] = jnp.zeros_like(level_sums)

    def weigh(plane, col_log, positive):
        cols = cols_of(plane)
        names = ids(plane)
        col_half = col_log + 1.0

        def weight_block(here, positive):
            value = logits[here, cols]
            hit = partner_col[here, 0:1] == names
            slope = (
                jnp.exp2(value - row_col[here, 0:1]) + jnp.exp2(value - col_half) - jnp.where(hit, 1.0, 0.0)
            )
            logits[here, cols] = slope
            weights[here, cols] = slope.astype(BF16)
            return positive + jnp.sum(jnp.where(hit, value, 0.0).reshape(step // 8, 8, span), axis=0)

        return by_rows(weight_block, positive)

    def time_partials(plane):
        stage[...] = lax.dot_general(weights[:, plane * span:(plane + 1) * span], notes_ref[...],
                                     (((0,), (0,)), ((), ())), preferred_element_type=F32)

        def share_time(s):
            peer = plane_peer(s)
            time_out[plane, peer] = stage[pl.ds(pl.multiple_of(peer * own, own), own)].astype(BF16)
            send(time_out.at[plane, peer], time_in.at[plane, q], t_send.at[plane, peer], t_recv.at[plane, q],
                 in_plane(peer))

        each(nq, share_time)
        part[plane] = stage[pl.ds(pl.multiple_of(q * own, own), own)]

    def add_levels(plane, days):
        cols = cols_of(plane)

        def level_block(here, _):
            value = logits[here, cols]
            distance = gap(here, days)
            for level in range(levels):
                picked = value if level == 0 else jnp.where(distance >= F32(BUCKET_DAYS * level), value, 0.0)
                level_sums[level] += jnp.sum(picked.reshape(step // 8, 8, span), axis=0)
            return 0

        by_rows(level_block, 0)

    far_log = cols_done(1, far_cols)
    positive = weigh(1, far_log, jnp.zeros((8, span), F32))
    time_partials(1)
    note_own[...] = jnp.dot(weights[:, span:2 * span], planes[1], preferred_element_type=F32)
    add_levels(1, far_days)
    near_log = cols_done(0, near_cols)
    positive = weigh(0, near_log, positive)

    note_own[...] += jnp.dot(weights[:, 0:span], planes[0], preferred_element_type=F32)

    def chunk(k, which):
        return pl.ds(pl.multiple_of((2 * k + which) * own, own), own)

    def share_core(s):
        k = lax.rem(line + 2 * s - 1 - (2 * s - 1) // nz * (nz - 1), nz)
        send(note_own.at[chunk(k, 1 - core)], note_near.at[k], n_send.at[k], n_recv.at[k],
             (outer_id, 2 * line + 1 - core))

    each(nz + 1, share_core)
    add_levels(0, near_days)

    above = jnp.sum(level_sums[...], axis=1)
    below = jnp.concatenate([above[1:], jnp.zeros((1, span), F32)], axis=0)
    loss = F32(LN2) * (
        (0.5 / group) * jnp.sum(row_log)
        + (0.5 / (2 * nq)) * (jnp.sum(near_log) + jnp.sum(far_log))
        - jnp.sum(positive)
    )
    buckets = jnp.sum(above - below, axis=1, keepdims=True)
    across_lanes = jnp.where(
        lax.broadcasted_iota(jnp.int32, (levels, wide), 0) == lax.broadcasted_iota(jnp.int32, (levels, wide), 1),
        buckets, 0.0)
    at_loss = lax.broadcasted_iota(jnp.int32, (1, wide), 1) == levels
    ring_sums[ring_id] = jnp.sum(across_lanes, axis=0, keepdims=True) + jnp.where(at_loss, loss, 0.0)

    def share_sums(s):
        peer = ring_peer(s)
        send(ring_sums.at[ring_id], ring_sums.at[ring_id], a_send.at[peer], a_recv.at[ring_id], on_ring(peer))

    each(2 * group, share_sums)

    half, odd = line // 2, line % 2
    beside = (outer_id, 2 * (2 * half + 1 - odd) + core)

    def share_pair(j, _):
        k = 2 * j + 1 - odd
        wait_in(note_near.at[k], n_recv.at[k])
        note_out[j] = (note_own[chunk(k, core)] + note_near[k]).astype(BF16)
        send(note_out.at[j], note_in.at[j], m_send.at[j], m_recv.at[j], beside)
        return 0

    lax.fori_loop(0, nz // 2, share_pair, 0)

    def keep_pair(j, _):
        k = 2 * j + odd
        wait_in(note_near.at[k], n_recv.at[k])
        note_near[k] += note_own[chunk(k, core)]
        return 0

    lax.fori_loop(0, nz // 2, keep_pair, 0)

    def share_line(s):
        j = lax.rem(half + s, nz // 2)
        k = 2 * j + odd
        wait_in(note_in.at[j], m_recv.at[j])
        pair_out[j] = (note_near[k] + note_in[j].astype(F32)).astype(BF16)
        send(pair_out.at[j], pair_in.at[half], p_send.at[j], p_recv.at[half], (outer_id, 2 * k + core))

    def time_arrive(plane):
        def one(s):
            peer = plane_peer(s)
            wait_in(time_in.at[plane, peer], t_recv.at[plane, peer])
            part[plane] += time_in[plane, peer].astype(F32)
        each(nq, one)

    time_arrive(1)
    far_out[...] = part[1].astype(BF16)
    send(far_out, far_in, t_send.at[1, q], t_recv.at[1, q], across)
    each(nz // 2, share_line)
    time_partials(0)

    def sums_in(s):
        peer = ring_peer(s)
        wait_in(ring_sums.at[peer], a_recv.at[peer])

    each(2 * group, sums_in)
    plane_sums[q] = functools.reduce(jnp.add, [ring_sums[k] for k in range(2 * group)])

    def share_plane_sums(s):
        peer = plane_peer(s)
        send(plane_sums.at[q], plane_sums.at[q], b_send.at[peer], b_recv.at[q], in_plane(peer))

    each(nq, share_plane_sums)
    time_arrive(0)

    factor = scale_ref[...] * F32(1.0 / math.sqrt(depth))
    wait_in(note_in.at[half], m_recv.at[half])
    note_near[line] += note_in[half].astype(F32)

    def note_arrive(s):
        j = lax.rem(half + s, nz // 2)
        wait_in(pair_in.at[j], p_recv.at[j])
        note_near[line] += pair_in[j].astype(F32)

    each(nz // 2, note_arrive)
    note_grad_ref[...] = factor * note_near[line]

    def plane_sums_in(s):
        peer = plane_peer(s)
        wait_in(plane_sums.at[peer], b_recv.at[peer])

    each(nq, plane_sums_in)
    summary_ref[...] = functools.reduce(jnp.add, [plane_sums[k] for k in range(nq)]) * F32(1.0 / (rows * 2 * nq))
    wait_in(far_in, t_recv.at[1, q])
    time_grad_ref[...] = factor * (part[0] + far_in[...].astype(F32))

    wait_out(shards.at[0, q], g_send.at[1, q])
    wait_out(shard_days.at[0, q], d_send.at[1, q])
    wait_out(far_out, t_send.at[1, q])

    def plane_left(s):
        peer = plane_peer(s)
        for plane in range(2):
            wait_out(shards.at[plane, q], g_send.at[plane, peer])
            wait_out(shard_days.at[plane, q], d_send.at[plane, peer])
            wait_out(col_stats.at[plane, q], c_send.at[plane, peer])
            wait_out(time_out.at[plane, peer], t_send.at[plane, peer])
        wait_out(plane_sums.at[q], b_send.at[peer])

    def line_left(s):
        j = lax.rem(half + s, nz // 2)
        wait_out(pair_out.at[j], p_send.at[j])

    for plane in range(2):
        wait_out(col_far.at[plane], f_send.at[plane])
    each(nq, plane_left)
    each(group, lambda s: wait_out(row_stats.at[inner_id], r_send.at[inner_peer(s)]))
    each(2 * group, lambda s: wait_out(ring_sums.at[ring_id], a_send.at[ring_peer(s)]))
    each(nz + 1, lambda s: wait_out(note_near.at[0], n_send.at[lax.rem(line + s, nz)]))
    each(nz // 2, line_left)
    lax.fori_loop(0, nz // 2, lambda j, _: wait_out(note_out.at[j], m_send.at[j]) or 0, 0)


def hand_over(note_ref, time_ref, summary_ref, loss_ref, bias_ref, note_out, time_out):
    levels = bias_ref.shape[0]
    note_out[...] = note_ref[...]
    time_out[...] = time_ref[...]
    bias_ref[...] = summary_ref[0, 0:levels]
    loss_ref[...] = summary_ref[0, levels:levels + 1]


def body(notes, timelines, partner, note_days, time_days, logit_scale, bias):
    rows, depth = notes.shape
    own = timelines.shape[0]
    nq = lax.axis_size("outer") // 2
    nz = lax.axis_size("inner") // 2
    ny = 2 ** (int(math.log2(nq)) // 2)
    span = nq * own
    group = 2 * nz
    levels = bias.shape[0]
    wide = 128
    vmem, anywhere = pl.BlockSpec(memory_space=pltpu.VMEM), pl.BlockSpec(memory_space=pltpu.HBM)
    dma = pltpu.SemaphoreType.DMA
    grads = jax.ShapeDtypeStruct((own, depth), F32)
    note_grad, time_grad, summary = pl.pallas_call(
        functools.partial(kernel, (nq // ny, ny, nz)),
        out_shape=(grads, grads, jax.ShapeDtypeStruct((1, wide), F32)),
        in_specs=[anywhere] * 7,
        out_specs=(vmem,) * 3,
        scratch_shapes=[
            pltpu.VMEM((1, 1), F32),
            pltpu.SMEM((levels,), F32),
            pltpu.VMEM((rows, depth), BF16),
            pltpu.VMEM((rows,), jnp.int32),
            pltpu.VMEM((rows,), jnp.int32),
            pltpu.VMEM((2, nq, own, depth), BF16),
            pltpu.VMEM((2, nq, 1, own), jnp.int32),
            pltpu.VMEM((span, depth), F32),
            pltpu.VMEM((2, span, depth), BF16),
            pltpu.VMEM((rows, 2 * span), F32),
            pltpu.VMEM((rows, span), F32),
            pltpu.VMEM((rows, 2 * span), BF16),
            pltpu.VMEM((rows, wide), F32),
            pltpu.VMEM((rows, wide), F32),
            pltpu.VMEM((rows, wide), F32),
            pltpu.VMEM((2, rows, wide), F32),
            pltpu.VMEM((group, 1, rows), F32),
            pltpu.VMEM((2, nq, 1, span), F32),
            pltpu.VMEM((4, 1, span), F32),
            pltpu.VMEM((2, own, depth), F32),
            pltpu.VMEM((2, nq, own, depth), BF16),
            pltpu.VMEM((2, nq, own, depth), BF16),
            pltpu.VMEM((own, depth), BF16),
            pltpu.VMEM((own, depth), BF16),
            pltpu.VMEM((nz, own, depth), F32),
            pltpu.VMEM((nz // 2, own, depth), BF16),
            pltpu.VMEM((nz // 2, own, depth), BF16),
            pltpu.VMEM((nz // 2, own, depth), BF16),
            pltpu.VMEM((nz // 2, own, depth), BF16),
            pltpu.VMEM((rows, depth), F32),
            pltpu.VMEM((levels, 8, span), F32),
            pltpu.VMEM((2 * group, 1, wide), F32),
            pltpu.VMEM((nq, 1, wide), F32),
            dma((7,)),
            dma((2, nq)), dma((2, nq)), dma((2, nq)), dma((2, nq)),
            dma((group,)), dma((group,)), dma((2, nq)), dma((2, nq)), dma((2,)), dma((2,)),
            dma((2, nq)), dma((2, nq)),
            dma((nz,)), dma((nz,)), dma((nz // 2,)), dma((nz // 2,)), dma((nz // 2,)), dma((nz // 2,)),
            dma((2 * group,)), dma((2 * group,)), dma((nq,)), dma((nq,)),
        ],
        compiler_params=pltpu.CompilerParams(
            collective_id=0, has_side_effects=True, vmem_limit_bytes=56 * 2**20
        ),
    )(
        logit_scale.reshape(1, 1), bias, notes, timelines,
        time_days.reshape(1, own), note_days, partner,
    )
    mean_loss, bias_grad, note_grad, time_grad = pl.pallas_call(
        hand_over,
        out_shape=(jax.ShapeDtypeStruct((1,), F32), jax.ShapeDtypeStruct((levels,), F32), grads, grads),
        in_specs=[vmem] * 3,
        out_specs=(vmem,) * 4,
    )(note_grad, time_grad, summary)
    return (mean_loss, bias_grad, note_grad, time_grad)


def solution(mesh):
    placed = (
        P("outer", None),
        P(("outer", "inner"), None),
        P("outer"),
        P("outer"),
        P(("outer", "inner")),
        P(),
        P(),
    )
    return jax.shard_map(
        body,
        mesh=mesh,
        in_specs=placed,
        out_specs=(P(), P(), P(("outer", "inner"), None), P(("outer", "inner"), None)),
        check_vma=False,
    )
```

```python
import functools
import math

import jax
import jax.numpy as jnp
from jax import lax
from jax.experimental import pallas as pl
from jax.experimental.pallas import tpu as pltpu
from jax.sharding import PartitionSpec as P

BUCKET_DAYS = 30
LOG2E = math.log2(math.e)
LN2 = math.log(2.0)
MESH = pl.DeviceIdType.MESH
F32 = jnp.float32
BF16 = jnp.bfloat16


def log2_sum(parts):
    peak = functools.reduce(jnp.maximum, parts)
    total = functools.reduce(jnp.add, [jnp.exp2(part - peak) for part in parts])
    return peak + jnp.log2(total)


def spread_rows(row, width):
    return jnp.broadcast_to(row, (width, row.shape[1])).T


def kernel(
    sizes,
    scale_any, bias_any, notes_any, time_any, when_any, note_when_any, partner_any,
    note_grad_ref, time_grad_ref, summary_ref,
    scale_ref, bias_ref, notes_ref, note_when_ref, partner_ref,
    shards, shard_days, stage, planes, logits, raws, weights, when_col, partner_col, row_col, spare,
    row_stats, col_stats, col_far, part, time_out, time_in, far_out, far_in,
    note_near, note_out, note_in, pair_out, pair_in, note_own, level_sums, ring_sums, plane_sums,
    l_sem, g_send, g_recv, d_send, d_recv, r_send, r_recv, c_send, c_recv, f_send, f_recv, t_send, t_recv,
    n_send, n_recv, m_send, m_recv, p_send, p_recv, a_send, a_recv, b_send, b_recv,
):
    nx, ny, nz = sizes
    nq, group = nx * ny, 2 * nz
    rows, depth = notes_ref.shape
    own = time_any.shape[0]
    span = nq * own
    step = min(128, rows)
    blocks = rows // step
    wide = when_col.shape[1]
    levels = bias_ref.shape[0]

    outer_id, inner_id = lax.axis_index("outer"), lax.axis_index("inner")
    q, far = outer_id // 2, outer_id % 2
    qx, qy = q // ny, q % ny
    line, core = inner_id // 2, inner_id % 2
    ring_id = far * group + inner_id

    def plane_peer(s):
        return lax.rem(qx + s // ny, nx) * ny + lax.rem(qy + s % ny, ny)

    def in_plane(peer):
        return (peer * 2 + far, inner_id)

    across = (q * 2 + 1 - far, inner_id)

    def inner_peer(s):
        return lax.rem(inner_id + s, group)

    def ring_peer(s):
        return lax.rem(ring_id + s, 2 * group)

    def on_ring(peer):
        return (q * 2 + peer // group, peer % group)

    def send(src, dst, send_sem, recv_sem, device):
        pltpu.make_async_remote_copy(
            src_ref=src, dst_ref=dst, send_sem=send_sem, recv_sem=recv_sem,
            device_id=device, device_id_type=MESH,
        ).start()

    def wait_in(dst, recv_sem):
        pltpu.make_async_copy(dst, dst, recv_sem).wait()

    wait_out = wait_in

    def each(count, one):
        def run(s, _):
            one(s)
            return 0
        lax.fori_loop(1, count, run, 0)

    barrier = pltpu.get_barrier_semaphore()

    def hello(device):
        pl.semaphore_signal(barrier, inc=1, device_id=device, device_id_type=MESH)

    def hello_far(s, _):
        hello((q * 2 + 1 - far, inner_peer(s)))
        return 0

    lax.fori_loop(0, group, hello_far, 0)
    each(group, lambda s: hello((outer_id, inner_peer(s))))
    each(nq, lambda s: hello(in_plane(plane_peer(s))))

    loads = [
        pltpu.make_async_copy(src, dst, l_sem.at[k])
        for k, (src, dst) in enumerate((
            (time_any, shards.at[0, q]), (when_any, shard_days.at[0, q]), (scale_any, scale_ref), (bias_any, bias_ref),
            (note_when_any, note_when_ref), (partner_any, partner_ref), (notes_any, notes_ref),
        ))
    ]
    for load in loads:
        load.start()
    for load in loads[:2]:
        load.wait()
    pl.semaphore_wait(barrier, (nq - 1) + (2 * group - 1))

    send(shards.at[0, q], shards.at[1, q], g_send.at[1, q], g_recv.at[1, q], across)
    send(shard_days.at[0, q], shard_days.at[1, q], d_send.at[1, q], d_recv.at[1, q], across)

    def share(plane):
        def one(s):
            peer = plane_peer(s)
            send(shard_days.at[plane, q], shard_days.at[plane, q], d_send.at[plane, peer], d_recv.at[plane, q],
                 in_plane(peer))
            send(shards.at[plane, q], shards.at[plane, q], g_send.at[plane, peer], g_recv.at[plane, q], in_plane(peer))
        each(nq, one)

    share(0)
    for load in loads[2:]:
        load.wait()
    scale = scale_ref[...] * F32(LOG2E / math.sqrt(depth))
    lane = lax.broadcasted_iota(jnp.int32, (1, span), 1)
    lane_q = ((lane.astype(F32) + 0.5) * F32(1.0 / own)).astype(jnp.int32)
    lane_r = lane - lane_q * own
    when_col[...] = spread_rows(note_when_ref[...].reshape(1, rows).astype(F32), wide)
    partner_col[...] = spread_rows(partner_ref[...].reshape(1, rows).astype(F32), wide)
    place = jnp.where(lax.broadcasted_iota(jnp.int32, (own, span), 0) == lane_r, 1.0, 0.0).astype(BF16)

    def plane_days(plane):
        days = jnp.concatenate([shard_days[plane, k] for k in range(nq)], axis=0).astype(F32)
        high = jnp.floor(days * F32(1.0 / 16.0))
        low = days - high * 16.0
        placed = 16.0 * jnp.dot(high.astype(BF16), place, preferred_element_type=F32) + jnp.dot(
            low.astype(BF16), place, preferred_element_type=F32)
        mine = lax.broadcasted_iota(jnp.int32, (nq, span), 0) == lane_q
        return jnp.sum(jnp.where(mine, placed, 0.0), axis=0, keepdims=True)

    def gap(here, days):
        return jnp.abs(when_col[here, 0:1] - days)

    def ids(plane):
        zone = far if plane == 0 else 1 - far
        return (((lane_q * 2 + zone) * group + inner_id) * own + lane_r).astype(F32)

    def by_rows(one, start):
        def run(block, carry):
            return one(pl.ds(pl.multiple_of(block * step, step), step), carry)
        return lax.fori_loop(0, blocks, run, start)

    def cols_of(plane):
        return pl.ds(plane * span, span)

    def days_in(plane):
        def one(s):
            peer = plane_peer(s)
            wait_in(shard_days.at[plane, peer], d_recv.at[plane, peer])
        each(nq, one)
        days = plane_days(plane)

        def offset_block(here, _):
            distance = gap(here, days)
            offset = jnp.full((step, span), bias_ref[0] * F32(LOG2E), F32)
            for level in range(1, levels):
                offset = jnp.where(distance >= F32(BUCKET_DAYS * level), bias_ref[level] * F32(LOG2E), offset)
            logits[here, cols_of(plane)] = offset
            return 0

        by_rows(offset_block, 0)
        return days

    def plane_in(plane):
        def one(s):
            peer = plane_peer(s)
            wait_in(shards.at[plane, peer], g_recv.at[plane, peer])
        each(nq, one)

        def settle(k, _):
            stage[pl.ds(pl.multiple_of(k * own, own), own)] = shards[plane, k].astype(F32)
            return 0
        lax.fori_loop(0, nq, settle, 0)
        planes[plane] = stage[...].astype(BF16)
        cols = cols_of(plane)

        raws[...] = lax.dot_general(notes_ref[...], planes[plane], (((1,), (1,)), ((), ())),
                                    preferred_element_type=F32)

        def logit_block(here, col_peak):
            value = raws[here] * scale + logits[here, cols]
            logits[here, cols] = value
            peak = jnp.max(value, axis=1, keepdims=True)
            total = jnp.sum(jnp.exp2(value - peak), axis=1, keepdims=True)
            spare[plane, here] = jnp.broadcast_to(peak + jnp.log2(total), (step, wide))
            return jnp.maximum(col_peak, jnp.max(value, axis=0, keepdims=True))

        col_peak = by_rows(logit_block, jnp.full((1, span), -jnp.inf, F32))

        def col_block(here, total):
            return total + jnp.sum(jnp.exp2(logits[here, cols] - col_peak), axis=0, keepdims=True)

        col_stats[plane, q] = col_peak + jnp.log2(by_rows(col_block, jnp.zeros((1, span), F32)))

        def share_cols(s):
            peer = plane_peer(s)
            send(col_stats.at[plane, q], col_stats.at[plane, q], c_send.at[plane, peer], c_recv.at[plane, q],
                 in_plane(peer))
        each(nq, share_cols)

    def cols_in(plane):
        def one(s):
            peer = plane_peer(s)
            wait_in(col_stats.at[plane, peer], c_recv.at[plane, peer])
        each(nq, one)
        near = log2_sum([col_stats[plane, k] for k in range(nq)])
        col_far[plane] = near
        send(col_far.at[plane], col_far.at[2 + 1 - plane], f_send.at[plane], f_recv.at[1 - plane], across)
        return near

    def cols_done(plane, near):
        wait_in(col_far.at[2 + plane], f_recv.at[plane])
        return log2_sum([near, col_far[2 + plane]])

    near_days = days_in(0)
    wait_in(shards.at[1, q], g_recv.at[1, q])
    wait_in(shard_days.at[1, q], d_recv.at[1, q])
    share(1)
    plane_in(0)
    far_days = days_in(1)
    near_cols = cols_in(0)
    plane_in(1)

    row_stats[inner_id] = log2_sum([spare[0], spare[1]]).T[0:1]

    def share_rows(s):
        peer = inner_peer(s)
        send(row_stats.at[inner_id], row_stats.at[inner_id], r_send.at[peer], r_recv.at[inner_id], (outer_id, peer))

    each(group, share_rows)
    far_cols = cols_in(1)

    def rows_in(s):
        peer = inner_peer(s)
        wait_in(row_stats.at[peer], r_recv.at[peer])

    each(group, rows_in)
    row_log = log2_sum([row_stats[k] for k in range(group)])
    row_col[...] = spread_rows(row_log + 1.0, wide)
    level_sums[...] = jnp.zeros_like(level_sums)

    def weigh(plane, col_log, positive):
        cols = cols_of(plane)
        names = ids(plane)
        col_half = col_log + 1.0

        def weight_block(here, positive):
            value = logits[here, cols]
            hit = partner_col[here, 0:1] == names
            slope = (
                jnp.exp2(value - row_col[here, 0:1]) + jnp.exp2(value - col_half) - jnp.where(hit, 1.0, 0.0)
            )
            logits[here, cols] = slope
            weights[here, cols] = slope.astype(BF16)
            return positive + jnp.sum(jnp.where(hit, value, 0.0).reshape(step // 8, 8, span), axis=0)

        return by_rows(weight_block, positive)

    def time_partials(plane):
        stage[...] = lax.dot_general(weights[:, plane * span:(plane + 1) * span], notes_ref[...],
                                     (((0,), (0,)), ((), ())), preferred_element_type=F32)

        def share_time(s):
            peer = plane_peer(s)
            time_out[plane, peer] = stage[pl.ds(pl.multiple_of(peer * own, own), own)].astype(BF16)
            send(time_out.at[plane, peer], time_in.at[plane, q], t_send.at[plane, peer], t_recv.at[plane, q],
                 in_plane(peer))

        each(nq, share_time)
        part[plane] = stage[pl.ds(pl.multiple_of(q * own, own), own)]

    def add_levels(plane, days):
        cols = cols_of(plane)

        def level_block(here, _):
            value = logits[here, cols]
            distance = gap(here, days)
            for level in range(levels):
                picked = value if level == 0 else jnp.where(distance >= F32(BUCKET_DAYS * level), value, 0.0)
                level_sums[level] += jnp.sum(picked.reshape(step // 8, 8, span), axis=0)
            return 0

        by_rows(level_block, 0)

    far_log = cols_done(1, far_cols)
    positive = weigh(1, far_log, jnp.zeros((8, span), F32))
    time_partials(1)
    note_own[...] = jnp.dot(weights[:, span:2 * span], planes[1], preferred_element_type=F32)
    add_levels(1, far_days)
    near_log = cols_done(0, near_cols)
    positive = weigh(0, near_log, positive)

    note_own[...] += jnp.dot(weights[:, 0:span], planes[0], preferred_element_type=F32)

    def chunk(k, which):
        return pl.ds(pl.multiple_of((2 * k + which) * own, own), own)

    def share_core(s):
        k = lax.rem(line + 2 * s - 1 - (2 * s - 1) // nz * (nz - 1), nz)
        send(note_own.at[chunk(k, 1 - core)], note_near.at[k], n_send.at[k], n_recv.at[k],
             (outer_id, 2 * line + 1 - core))

    each(nz + 1, share_core)
    half, odd = line // 2, line % 2
    beside = (outer_id, 2 * (2 * half + 1 - odd) + core)

    def share_pair(j, _):
        k = 2 * j + 1 - odd
        wait_in(note_near.at[k], n_recv.at[k])
        note_out[j] = (note_own[chunk(k, core)] + note_near[k]).astype(BF16)
        send(note_out.at[j], note_in.at[j], m_send.at[j], m_recv.at[j], beside)
        return 0

    lax.fori_loop(0, nz // 2, share_pair, 0)

    add_levels(0, near_days)

    above = jnp.sum(level_sums[...], axis=1)
    below = jnp.concatenate([above[1:], jnp.zeros((1, span), F32)], axis=0)
    loss = F32(LN2) * (
        (0.5 / group) * jnp.sum(row_log)
        + (0.5 / (2 * nq)) * (jnp.sum(near_log) + jnp.sum(far_log))
        - jnp.sum(positive)
    )
    buckets = jnp.sum(above - below, axis=1, keepdims=True)
    across_lanes = jnp.where(
        lax.broadcasted_iota(jnp.int32, (levels, wide), 0) == lax.broadcasted_iota(jnp.int32, (levels, wide), 1),
        buckets, 0.0)
    at_loss = lax.broadcasted_iota(jnp.int32, (1, wide), 1) == levels
    ring_sums[ring_id] = jnp.sum(across_lanes, axis=0, keepdims=True) + jnp.where(at_loss, loss, 0.0)

    def share_sums(s):
        peer = ring_peer(s)
        send(ring_sums.at[ring_id], ring_sums.at[ring_id], a_send.at[peer], a_recv.at[ring_id], on_ring(peer))

    each(2 * group, share_sums)

    def keep_pair(j, _):
        k = 2 * j + odd
        wait_in(note_near.at[k], n_recv.at[k])
        note_near[k] += note_own[chunk(k, core)]
        return 0

    lax.fori_loop(0, nz // 2, keep_pair, 0)

    def share_line(s):
        j = lax.rem(half + s, nz // 2)
        k = 2 * j + odd
        wait_in(note_in.at[j], m_recv.at[j])
        pair_out[j] = (note_near[k] + note_in[j].astype(F32)).astype(BF16)
        send(pair_out.at[j], pair_in.at[half], p_send.at[j], p_recv.at[half], (outer_id, 2 * k + core))

    def time_arrive(plane):
        def one(s):
            peer = plane_peer(s)
            wait_in(time_in.at[plane, peer], t_recv.at[plane, peer])
            part[plane] += time_in[plane, peer].astype(F32)
        each(nq, one)

    time_arrive(1)
    far_out[...] = part[1].astype(BF16)
    send(far_out, far_in, t_send.at[1, q], t_recv.at[1, q], across)
    each(nz // 2, share_line)
    time_partials(0)

    def sums_in(s):
        peer = ring_peer(s)
        wait_in(ring_sums.at[peer], a_recv.at[peer])

    each(2 * group, sums_in)
    plane_sums[q] = functools.reduce(jnp.add, [ring_sums[k] for k in range(2 * group)])

    def share_plane_sums(s):
        peer = plane_peer(s)
        send(plane_sums.at[q], plane_sums.at[q], b_send.at[peer], b_recv.at[q], in_plane(peer))

    each(nq, share_plane_sums)
    time_arrive(0)

    factor = scale_ref[...] * F32(1.0 / math.sqrt(depth))
    wait_in(note_in.at[half], m_recv.at[half])
    note_near[line] += note_in[half].astype(F32)

    def note_arrive(s):
        j = lax.rem(half + s, nz // 2)
        wait_in(pair_in.at[j], p_recv.at[j])
        note_near[line] += pair_in[j].astype(F32)

    each(nz // 2, note_arrive)
    note_grad_ref[...] = factor * note_near[line]

    def plane_sums_in(s):
        peer = plane_peer(s)
        wait_in(plane_sums.at[peer], b_recv.at[peer])

    each(nq, plane_sums_in)
    summary_ref[...] = functools.reduce(jnp.add, [plane_sums[k] for k in range(nq)]) * F32(1.0 / (rows * 2 * nq))
    wait_in(far_in, t_recv.at[1, q])
    time_grad_ref[...] = factor * (part[0] + far_in[...].astype(F32))

    wait_out(shards.at[0, q], g_send.at[1, q])
    wait_out(shard_days.at[0, q], d_send.at[1, q])
    wait_out(far_out, t_send.at[1, q])

    def plane_left(s):
        peer = plane_peer(s)
        for plane in range(2):
            wait_out(shards.at[plane, q], g_send.at[plane, peer])
            wait_out(shard_days.at[plane, q], d_send.at[plane, peer])
            wait_out(col_stats.at[plane, q], c_send.at[plane, peer])
            wait_out(time_out.at[plane, peer], t_send.at[plane, peer])
        wait_out(plane_sums.at[q], b_send.at[peer])

    def line_left(s):
        j = lax.rem(half + s, nz // 2)
        wait_out(pair_out.at[j], p_send.at[j])

    for plane in range(2):
        wait_out(col_far.at[plane], f_send.at[plane])
    each(nq, plane_left)
    each(group, lambda s: wait_out(row_stats.at[inner_id], r_send.at[inner_peer(s)]))
    each(2 * group, lambda s: wait_out(ring_sums.at[ring_id], a_send.at[ring_peer(s)]))
    each(nz + 1, lambda s: wait_out(note_near.at[0], n_send.at[lax.rem(line + s, nz)]))
    each(nz // 2, line_left)
    lax.fori_loop(0, nz // 2, lambda j, _: wait_out(note_out.at[j], m_send.at[j]) or 0, 0)


def hand_over(note_ref, time_ref, summary_ref, loss_ref, bias_ref, note_out, time_out):
    levels = bias_ref.shape[0]
    note_out[...] = note_ref[...]
    time_out[...] = time_ref[...]
    bias_ref[...] = summary_ref[0, 0:levels]
    loss_ref[...] = summary_ref[0, levels:levels + 1]


def body(notes, timelines, partner, note_days, time_days, logit_scale, bias):
    rows, depth = notes.shape
    own = timelines.shape[0]
    nq = lax.axis_size("outer") // 2
    nz = lax.axis_size("inner") // 2
    ny = 2 ** (int(math.log2(nq)) // 2)
    span = nq * own
    group = 2 * nz
    levels = bias.shape[0]
    wide = 128
    vmem, anywhere = pl.BlockSpec(memory_space=pltpu.VMEM), pl.BlockSpec(memory_space=pltpu.HBM)
    dma = pltpu.SemaphoreType.DMA
    grads = jax.ShapeDtypeStruct((own, depth), F32)
    note_grad, time_grad, summary = pl.pallas_call(
        functools.partial(kernel, (nq // ny, ny, nz)),
        out_shape=(grads, grads, jax.ShapeDtypeStruct((1, wide), F32)),
        in_specs=[anywhere] * 7,
        out_specs=(vmem,) * 3,
        scratch_shapes=[
            pltpu.VMEM((1, 1), F32),
            pltpu.SMEM((levels,), F32),
            pltpu.VMEM((rows, depth), BF16),
            pltpu.VMEM((rows,), jnp.int32),
            pltpu.VMEM((rows,), jnp.int32),
            pltpu.VMEM((2, nq, own, depth), BF16),
            pltpu.VMEM((2, nq, 1, own), jnp.int32),
            pltpu.VMEM((span, depth), F32),
            pltpu.VMEM((2, span, depth), BF16),
            pltpu.VMEM((rows, 2 * span), F32),
            pltpu.VMEM((rows, span), F32),
            pltpu.VMEM((rows, 2 * span), BF16),
            pltpu.VMEM((rows, wide), F32),
            pltpu.VMEM((rows, wide), F32),
            pltpu.VMEM((rows, wide), F32),
            pltpu.VMEM((2, rows, wide), F32),
            pltpu.VMEM((group, 1, rows), F32),
            pltpu.VMEM((2, nq, 1, span), F32),
            pltpu.VMEM((4, 1, span), F32),
            pltpu.VMEM((2, own, depth), F32),
            pltpu.VMEM((2, nq, own, depth), BF16),
            pltpu.VMEM((2, nq, own, depth), BF16),
            pltpu.VMEM((own, depth), BF16),
            pltpu.VMEM((own, depth), BF16),
            pltpu.VMEM((nz, own, depth), F32),
            pltpu.VMEM((nz // 2, own, depth), BF16),
            pltpu.VMEM((nz // 2, own, depth), BF16),
            pltpu.VMEM((nz // 2, own, depth), BF16),
            pltpu.VMEM((nz // 2, own, depth), BF16),
            pltpu.VMEM((rows, depth), F32),
            pltpu.VMEM((levels, 8, span), F32),
            pltpu.VMEM((2 * group, 1, wide), F32),
            pltpu.VMEM((nq, 1, wide), F32),
            dma((7,)),
            dma((2, nq)), dma((2, nq)), dma((2, nq)), dma((2, nq)),
            dma((group,)), dma((group,)), dma((2, nq)), dma((2, nq)), dma((2,)), dma((2,)),
            dma((2, nq)), dma((2, nq)),
            dma((nz,)), dma((nz,)), dma((nz // 2,)), dma((nz // 2,)), dma((nz // 2,)), dma((nz // 2,)),
            dma((2 * group,)), dma((2 * group,)), dma((nq,)), dma((nq,)),
        ],
        compiler_params=pltpu.CompilerParams(
            collective_id=0, has_side_effects=True, vmem_limit_bytes=56 * 2**20
        ),
    )(
        logit_scale.reshape(1, 1), bias, notes, timelines,
        time_days.reshape(1, own), note_days, partner,
    )
    mean_loss, bias_grad, note_grad, time_grad = pl.pallas_call(
        hand_over,
        out_shape=(jax.ShapeDtypeStruct((1,), F32), jax.ShapeDtypeStruct((levels,), F32), grads, grads),
        in_specs=[vmem] * 3,
        out_specs=(vmem,) * 4,
    )(note_grad, time_grad, summary)
    return (mean_loss, bias_grad, note_grad, time_grad)


def solution(mesh):
    placed = (
        P("outer", None),
        P(("outer", "inner"), None),
        P("outer"),
        P("outer"),
        P(("outer", "inner")),
        P(),
        P(),
    )
    return jax.shard_map(
        body,
        mesh=mesh,
        in_specs=placed,
        out_specs=(P(), P(), P(("outer", "inner"), None), P(("outer", "inner"), None)),
        check_vma=False,
    )
```

```python
import functools
import math

import jax
import jax.numpy as jnp
from jax import lax
from jax.experimental import pallas as pl
from jax.experimental.pallas import tpu as pltpu
from jax.sharding import PartitionSpec as P

BUCKET_DAYS = 30
LOG2E = math.log2(math.e)
LN2 = math.log(2.0)
MESH = pl.DeviceIdType.MESH
F32 = jnp.float32
BF16 = jnp.bfloat16


def log2_sum(parts):
    peak = functools.reduce(jnp.maximum, parts)
    total = functools.reduce(jnp.add, [jnp.exp2(part - peak) for part in parts])
    return peak + jnp.log2(total)


def spread_rows(row, width):
    return jnp.broadcast_to(row, (width, row.shape[1])).T


def kernel(
    sizes,
    scale_any, bias_any, notes_any, time_any, when_any, note_when_any, partner_any,
    note_grad_ref, time_grad_ref, summary_ref,
    scale_ref, bias_ref, notes_ref, note_when_ref, partner_ref,
    shards, shard_days, stage, planes, logits, raws, weights, when_col, partner_col, row_col, spare,
    row_stats, col_stats, col_far, part, time_out, time_in, far_out, far_in,
    note_near, note_out, note_in, pair_out, pair_in, note_own, level_sums, ring_sums, plane_sums,
    l_sem, g_send, g_recv, d_send, d_recv, r_send, r_recv, c_send, c_recv, f_send, f_recv, t_send, t_recv,
    n_send, n_recv, m_send, m_recv, p_send, p_recv, a_send, a_recv, b_send, b_recv,
):
    nx, ny, nz = sizes
    nq, group = nx * ny, 2 * nz
    rows, depth = notes_ref.shape
    own = time_any.shape[0]
    span = nq * own
    step = min(128, rows)
    blocks = rows // step
    wide = when_col.shape[1]
    levels = bias_ref.shape[0]

    outer_id, inner_id = lax.axis_index("outer"), lax.axis_index("inner")
    q, far = outer_id // 2, outer_id % 2
    qx, qy = q // ny, q % ny
    line, core = inner_id // 2, inner_id % 2
    ring_id = far * group + inner_id

    def plane_peer(s):
        return lax.rem(qx + s // ny, nx) * ny + lax.rem(qy + s % ny, ny)

    def in_plane(peer):
        return (peer * 2 + far, inner_id)

    across = (q * 2 + 1 - far, inner_id)

    def inner_peer(s):
        return lax.rem(inner_id + s, group)

    def ring_peer(s):
        return lax.rem(ring_id + s, 2 * group)

    def on_ring(peer):
        return (q * 2 + peer // group, peer % group)

    def send(src, dst, send_sem, recv_sem, device):
        pltpu.make_async_remote_copy(
            src_ref=src, dst_ref=dst, send_sem=send_sem, recv_sem=recv_sem,
            device_id=device, device_id_type=MESH,
        ).start()

    def wait_in(dst, recv_sem):
        pltpu.make_async_copy(dst, dst, recv_sem).wait()

    wait_out = wait_in

    def each(count, one):
        def run(s, _):
            one(s)
            return 0
        lax.fori_loop(1, count, run, 0)

    barrier = pltpu.get_barrier_semaphore()

    def hello(device):
        pl.semaphore_signal(barrier, inc=1, device_id=device, device_id_type=MESH)

    def hello_far(s, _):
        hello((q * 2 + 1 - far, inner_peer(s)))
        return 0

    lax.fori_loop(0, group, hello_far, 0)
    each(group, lambda s: hello((outer_id, inner_peer(s))))
    each(nq, lambda s: hello(in_plane(plane_peer(s))))

    loads = [
        pltpu.make_async_copy(src, dst, l_sem.at[k])
        for k, (src, dst) in enumerate((
            (time_any, shards.at[0, q]), (when_any, shard_days.at[0, q]), (scale_any, scale_ref), (bias_any, bias_ref),
            (note_when_any, note_when_ref), (partner_any, partner_ref), (notes_any, notes_ref),
        ))
    ]
    for load in loads:
        load.start()
    for load in loads[:2]:
        load.wait()
    pl.semaphore_wait(barrier, (nq - 1) + (2 * group - 1))

    send(shards.at[0, q], shards.at[1, q], g_send.at[1, q], g_recv.at[1, q], across)
    send(shard_days.at[0, q], shard_days.at[1, q], d_send.at[1, q], d_recv.at[1, q], across)

    def share(plane):
        def one(s):
            peer = plane_peer(s)
            send(shard_days.at[plane, q], shard_days.at[plane, q], d_send.at[plane, peer], d_recv.at[plane, q],
                 in_plane(peer))
            send(shards.at[plane, q], shards.at[plane, q], g_send.at[plane, peer], g_recv.at[plane, q], in_plane(peer))
        each(nq, one)

    share(0)
    for load in loads[2:]:
        load.wait()
    scale = scale_ref[...] * F32(LOG2E / math.sqrt(depth))
    lane = lax.broadcasted_iota(jnp.int32, (1, span), 1)
    lane_q = ((lane.astype(F32) + 0.5) * F32(1.0 / own)).astype(jnp.int32)
    lane_r = lane - lane_q * own
    when_col[...] = spread_rows(note_when_ref[...].reshape(1, rows).astype(F32), wide)
    partner_col[...] = spread_rows(partner_ref[...].reshape(1, rows).astype(F32), wide)
    place = jnp.where(lax.broadcasted_iota(jnp.int32, (own, span), 0) == lane_r, 1.0, 0.0).astype(BF16)

    def plane_days(plane):
        days = jnp.concatenate([shard_days[plane, k] for k in range(nq)], axis=0).astype(F32)
        high = jnp.floor(days * F32(1.0 / 16.0))
        low = days - high * 16.0
        placed = 16.0 * jnp.dot(high.astype(BF16), place, preferred_element_type=F32) + jnp.dot(
            low.astype(BF16), place, preferred_element_type=F32)
        mine = lax.broadcasted_iota(jnp.int32, (nq, span), 0) == lane_q
        return jnp.sum(jnp.where(mine, placed, 0.0), axis=0, keepdims=True)

    def gap(here, days):
        return jnp.abs(when_col[here, 0:1] - days)

    def ids(plane):
        zone = far if plane == 0 else 1 - far
        return (((lane_q * 2 + zone) * group + inner_id) * own + lane_r).astype(F32)

    def by_rows(one, start):
        def run(block, carry):
            return one(pl.ds(pl.multiple_of(block * step, step), step), carry)
        return lax.fori_loop(0, blocks, run, start)

    def cols_of(plane):
        return pl.ds(plane * span, span)

    def days_in(plane):
        def one(s):
            peer = plane_peer(s)
            wait_in(shard_days.at[plane, peer], d_recv.at[plane, peer])
        each(nq, one)
        days = plane_days(plane)

        def offset_block(here, _):
            distance = gap(here, days)
            offset = jnp.full((step, span), bias_ref[0] * F32(LOG2E), F32)
            for level in range(1, levels):
                offset = jnp.where(distance >= F32(BUCKET_DAYS * level), bias_ref[level] * F32(LOG2E), offset)
            logits[here, cols_of(plane)] = offset
            return 0

        by_rows(offset_block, 0)
        return days

    def plane_in(plane):
        def one(s):
            peer = plane_peer(s)
            wait_in(shards.at[plane, peer], g_recv.at[plane, peer])
        each(nq, one)

        planes[plane] = shards[plane].astype(F32).reshape(span, depth).astype(BF16)
        cols = cols_of(plane)

        raws[...] = lax.dot_general(notes_ref[...], planes[plane], (((1,), (1,)), ((), ())),
                                    preferred_element_type=F32)

        def logit_block(here, col_peak):
            value = raws[here] * scale + logits[here, cols]
            logits[here, cols] = value
            peak = jnp.max(value, axis=1, keepdims=True)
            total = jnp.sum(jnp.exp2(value - peak), axis=1, keepdims=True)
            spare[plane, here] = jnp.broadcast_to(peak + jnp.log2(total), (step, wide))
            return jnp.maximum(col_peak, jnp.max(value, axis=0, keepdims=True))

        col_peak = by_rows(logit_block, jnp.full((1, span), -jnp.inf, F32))

        def col_block(here, total):
            return total + jnp.sum(jnp.exp2(logits[here, cols] - col_peak), axis=0, keepdims=True)

        col_stats[plane, q] = col_peak + jnp.log2(by_rows(col_block, jnp.zeros((1, span), F32)))

        def share_cols(s):
            peer = plane_peer(s)
            send(col_stats.at[plane, q], col_stats.at[plane, q], c_send.at[plane, peer], c_recv.at[plane, q],
                 in_plane(peer))
        each(nq, share_cols)

    def cols_in(plane):
        def one(s):
            peer = plane_peer(s)
            wait_in(col_stats.at[plane, peer], c_recv.at[plane, peer])
        each(nq, one)
        near = log2_sum([col_stats[plane, k] for k in range(nq)])
        col_far[plane] = near
        send(col_far.at[plane], col_far.at[2 + 1 - plane], f_send.at[plane], f_recv.at[1 - plane], across)
        return near

    def cols_done(plane, near):
        wait_in(col_far.at[2 + plane], f_recv.at[plane])
        return log2_sum([near, col_far[2 + plane]])

    level_sums[...] = jnp.zeros_like(level_sums)
    near_days = days_in(0)
    wait_in(shards.at[1, q], g_recv.at[1, q])
    wait_in(shard_days.at[1, q], d_recv.at[1, q])
    share(1)
    plane_in(0)
    far_days = days_in(1)
    near_cols = cols_in(0)
    plane_in(1)

    row_stats[inner_id] = log2_sum([spare[0], spare[1]]).T[0:1]

    def share_rows(s):
        peer = inner_peer(s)
        send(row_stats.at[inner_id], row_stats.at[inner_id], r_send.at[peer], r_recv.at[inner_id], (outer_id, peer))

    each(group, share_rows)
    far_cols = cols_in(1)

    def rows_in(s):
        peer = inner_peer(s)
        wait_in(row_stats.at[peer], r_recv.at[peer])

    each(group, rows_in)
    row_log = log2_sum([row_stats[k] for k in range(group)])
    row_col[...] = spread_rows(row_log + 1.0, wide)

    def weigh(plane, col_log, positive):
        cols = cols_of(plane)
        names = ids(plane)
        col_half = col_log + 1.0

        def weight_block(here, positive):
            value = logits[here, cols]
            hit = partner_col[here, 0:1] == names
            slope = (
                jnp.exp2(value - row_col[here, 0:1]) + jnp.exp2(value - col_half) - jnp.where(hit, 1.0, 0.0)
            )
            logits[here, cols] = slope
            weights[here, cols] = slope.astype(BF16)
            return positive + jnp.sum(jnp.where(hit, value, 0.0).reshape(step // 8, 8, span), axis=0)

        return by_rows(weight_block, positive)

    def time_partials(plane):
        stage[...] = lax.dot_general(weights[:, plane * span:(plane + 1) * span], notes_ref[...],
                                     (((0,), (0,)), ((), ())), preferred_element_type=F32)

        def share_time(s):
            peer = plane_peer(s)
            time_out[plane, peer] = stage[pl.ds(pl.multiple_of(peer * own, own), own)].astype(BF16)
            send(time_out.at[plane, peer], time_in.at[plane, q], t_send.at[plane, peer], t_recv.at[plane, q],
                 in_plane(peer))

        each(nq, share_time)
        part[plane] = stage[pl.ds(pl.multiple_of(q * own, own), own)]

    def add_levels(plane, days):
        cols = cols_of(plane)

        def level_block(here, _):
            value = logits[here, cols]
            distance = gap(here, days)
            for level in range(levels):
                picked = value if level == 0 else jnp.where(distance >= F32(BUCKET_DAYS * level), value, 0.0)
                level_sums[level] += jnp.sum(picked.reshape(step // 8, 8, span), axis=0)
            return 0

        by_rows(level_block, 0)

    far_log = cols_done(1, far_cols)
    positive = weigh(1, far_log, jnp.zeros((8, span), F32))
    time_partials(1)
    note_own[...] = jnp.dot(weights[:, span:2 * span], planes[1], preferred_element_type=F32)
    add_levels(1, far_days)
    near_log = cols_done(0, near_cols)
    positive = weigh(0, near_log, positive)

    note_own[...] += jnp.dot(weights[:, 0:span], planes[0], preferred_element_type=F32)

    def chunk(k, which):
        return pl.ds(pl.multiple_of((2 * k + which) * own, own), own)

    def share_core(s):
        k = lax.rem(line + 2 * s - 1 - (2 * s - 1) // nz * (nz - 1), nz)
        send(note_own.at[chunk(k, 1 - core)], note_near.at[k], n_send.at[k], n_recv.at[k],
             (outer_id, 2 * line + 1 - core))

    each(nz + 1, share_core)
    half, odd = line // 2, line % 2
    beside = (outer_id, 2 * (2 * half + 1 - odd) + core)

    def share_pair(j, _):
        k = 2 * j + 1 - odd
        wait_in(note_near.at[k], n_recv.at[k])
        note_out[j] = (note_own[chunk(k, core)] + note_near[k]).astype(BF16)
        send(note_out.at[j], note_in.at[j], m_send.at[j], m_recv.at[j], beside)
        return 0

    lax.fori_loop(0, nz // 2, share_pair, 0)

    add_levels(0, near_days)

    above = jnp.sum(level_sums[...], axis=1)
    below = jnp.concatenate([above[1:], jnp.zeros((1, span), F32)], axis=0)
    loss = F32(LN2) * (
        (0.5 / group) * jnp.sum(row_log)
        + (0.5 / (2 * nq)) * (jnp.sum(near_log) + jnp.sum(far_log))
        - jnp.sum(positive)
    )
    buckets = jnp.sum(above - below, axis=1, keepdims=True)
    across_lanes = jnp.where(
        lax.broadcasted_iota(jnp.int32, (levels, wide), 0) == lax.broadcasted_iota(jnp.int32, (levels, wide), 1),
        buckets, 0.0)
    at_loss = lax.broadcasted_iota(jnp.int32, (1, wide), 1) == levels
    ring_sums[ring_id] = jnp.sum(across_lanes, axis=0, keepdims=True) + jnp.where(at_loss, loss, 0.0)

    def share_sums(s):
        peer = ring_peer(s)
        send(ring_sums.at[ring_id], ring_sums.at[ring_id], a_send.at[peer], a_recv.at[ring_id], on_ring(peer))

    each(2 * group, share_sums)

    def keep_pair(j, _):
        k = 2 * j + odd
        wait_in(note_near.at[k], n_recv.at[k])
        note_near[k] += note_own[chunk(k, core)]
        return 0

    lax.fori_loop(0, nz // 2, keep_pair, 0)

    def share_line(s):
        j = lax.rem(half + s, nz // 2)
        k = 2 * j + odd
        wait_in(note_in.at[j], m_recv.at[j])
        pair_out[j] = (note_near[k] + note_in[j].astype(F32)).astype(BF16)
        send(pair_out.at[j], pair_in.at[half], p_send.at[j], p_recv.at[half], (outer_id, 2 * k + core))

    def time_arrive(plane):
        def one(s):
            peer = plane_peer(s)
            wait_in(time_in.at[plane, peer], t_recv.at[plane, peer])
            part[plane] += time_in[plane, peer].astype(F32)
        each(nq, one)

    time_arrive(1)
    far_out[...] = part[1].astype(BF16)
    send(far_out, far_in, t_send.at[1, q], t_recv.at[1, q], across)
    each(nz // 2, share_line)
    time_partials(0)

    def sums_in(s):
        peer = ring_peer(s)
        wait_in(ring_sums.at[peer], a_recv.at[peer])

    each(2 * group, sums_in)
    plane_sums[q] = functools.reduce(jnp.add, [ring_sums[k] for k in range(2 * group)])

    def share_plane_sums(s):
        peer = plane_peer(s)
        send(plane_sums.at[q], plane_sums.at[q], b_send.at[peer], b_recv.at[q], in_plane(peer))

    each(nq, share_plane_sums)
    time_arrive(0)

    factor = scale_ref[...] * F32(1.0 / math.sqrt(depth))
    wait_in(note_in.at[half], m_recv.at[half])
    note_near[line] += note_in[half].astype(F32)

    def note_arrive(s):
        j = lax.rem(half + s, nz // 2)
        wait_in(pair_in.at[j], p_recv.at[j])
        note_near[line] += pair_in[j].astype(F32)

    each(nz // 2, note_arrive)
    note_grad_ref[...] = factor * note_near[line]

    def plane_sums_in(s):
        peer = plane_peer(s)
        wait_in(plane_sums.at[peer], b_recv.at[peer])

    each(nq, plane_sums_in)
    summary_ref[...] = functools.reduce(jnp.add, [plane_sums[k] for k in range(nq)]) * F32(1.0 / (rows * 2 * nq))
    wait_in(far_in, t_recv.at[1, q])
    time_grad_ref[...] = factor * (part[0] + far_in[...].astype(F32))

    wait_out(shards.at[0, q], g_send.at[1, q])
    wait_out(shard_days.at[0, q], d_send.at[1, q])
    wait_out(far_out, t_send.at[1, q])

    def plane_left(s):
        peer = plane_peer(s)
        for plane in range(2):
            wait_out(shards.at[plane, q], g_send.at[plane, peer])
            wait_out(shard_days.at[plane, q], d_send.at[plane, peer])
            wait_out(col_stats.at[plane, q], c_send.at[plane, peer])
            wait_out(time_out.at[plane, peer], t_send.at[plane, peer])
        wait_out(plane_sums.at[q], b_send.at[peer])

    def line_left(s):
        j = lax.rem(half + s, nz // 2)
        wait_out(pair_out.at[j], p_send.at[j])

    for plane in range(2):
        wait_out(col_far.at[plane], f_send.at[plane])
    each(nq, plane_left)
    each(group, lambda s: wait_out(row_stats.at[inner_id], r_send.at[inner_peer(s)]))
    each(2 * group, lambda s: wait_out(ring_sums.at[ring_id], a_send.at[ring_peer(s)]))
    each(nz + 1, lambda s: wait_out(note_near.at[0], n_send.at[lax.rem(line + s, nz)]))
    each(nz // 2, line_left)
    lax.fori_loop(0, nz // 2, lambda j, _: wait_out(note_out.at[j], m_send.at[j]) or 0, 0)


def hand_over(note_ref, time_ref, summary_ref, loss_ref, bias_ref, note_out, time_out):
    levels = bias_ref.shape[0]
    note_out[...] = note_ref[...]
    time_out[...] = time_ref[...]
    bias_ref[...] = summary_ref[0, 0:levels]
    loss_ref[...] = summary_ref[0, levels:levels + 1]


def body(notes, timelines, partner, note_days, time_days, logit_scale, bias):
    rows, depth = notes.shape
    own = timelines.shape[0]
    nq = lax.axis_size("outer") // 2
    nz = lax.axis_size("inner") // 2
    ny = 2 ** (int(math.log2(nq)) // 2)
    span = nq * own
    group = 2 * nz
    levels = bias.shape[0]
    wide = 128
    vmem, anywhere = pl.BlockSpec(memory_space=pltpu.VMEM), pl.BlockSpec(memory_space=pltpu.HBM)
    dma = pltpu.SemaphoreType.DMA
    grads = jax.ShapeDtypeStruct((own, depth), F32)
    note_grad, time_grad, summary = pl.pallas_call(
        functools.partial(kernel, (nq // ny, ny, nz)),
        out_shape=(grads, grads, jax.ShapeDtypeStruct((1, wide), F32)),
        in_specs=[anywhere] * 7,
        out_specs=(vmem,) * 3,
        scratch_shapes=[
            pltpu.VMEM((1, 1), F32),
            pltpu.SMEM((levels,), F32),
            pltpu.VMEM((rows, depth), BF16),
            pltpu.VMEM((rows,), jnp.int32),
            pltpu.VMEM((rows,), jnp.int32),
            pltpu.VMEM((2, nq, own, depth), BF16),
            pltpu.VMEM((2, nq, 1, own), jnp.int32),
            pltpu.VMEM((span, depth), F32),
            pltpu.VMEM((2, span, depth), BF16),
            pltpu.VMEM((rows, 2 * span), F32),
            pltpu.VMEM((rows, span), F32),
            pltpu.VMEM((rows, 2 * span), BF16),
            pltpu.VMEM((rows, wide), F32),
            pltpu.VMEM((rows, wide), F32),
            pltpu.VMEM((rows, wide), F32),
            pltpu.VMEM((2, rows, wide), F32),
            pltpu.VMEM((group, 1, rows), F32),
            pltpu.VMEM((2, nq, 1, span), F32),
            pltpu.VMEM((4, 1, span), F32),
            pltpu.VMEM((2, own, depth), F32),
            pltpu.VMEM((2, nq, own, depth), BF16),
            pltpu.VMEM((2, nq, own, depth), BF16),
            pltpu.VMEM((own, depth), BF16),
            pltpu.VMEM((own, depth), BF16),
            pltpu.VMEM((nz, own, depth), F32),
            pltpu.VMEM((nz // 2, own, depth), BF16),
            pltpu.VMEM((nz // 2, own, depth), BF16),
            pltpu.VMEM((nz // 2, own, depth), BF16),
            pltpu.VMEM((nz // 2, own, depth), BF16),
            pltpu.VMEM((rows, depth), F32),
            pltpu.VMEM((levels, 8, span), F32),
            pltpu.VMEM((2 * group, 1, wide), F32),
            pltpu.VMEM((nq, 1, wide), F32),
            dma((7,)),
            dma((2, nq)), dma((2, nq)), dma((2, nq)), dma((2, nq)),
            dma((group,)), dma((group,)), dma((2, nq)), dma((2, nq)), dma((2,)), dma((2,)),
            dma((2, nq)), dma((2, nq)),
            dma((nz,)), dma((nz,)), dma((nz // 2,)), dma((nz // 2,)), dma((nz // 2,)), dma((nz // 2,)),
            dma((2 * group,)), dma((2 * group,)), dma((nq,)), dma((nq,)),
        ],
        compiler_params=pltpu.CompilerParams(
            collective_id=0, has_side_effects=True, vmem_limit_bytes=56 * 2**20
        ),
    )(
        logit_scale.reshape(1, 1), bias, notes, timelines,
        time_days.reshape(1, own), note_days, partner,
    )
    mean_loss, bias_grad, note_grad, time_grad = pl.pallas_call(
        hand_over,
        out_shape=(jax.ShapeDtypeStruct((1,), F32), jax.ShapeDtypeStruct((levels,), F32), grads, grads),
        in_specs=[vmem] * 3,
        out_specs=(vmem,) * 4,
    )(note_grad, time_grad, summary)
    return (mean_loss, bias_grad, note_grad, time_grad)


def solution(mesh):
    placed = (
        P("outer", None),
        P(("outer", "inner"), None),
        P("outer"),
        P("outer"),
        P(("outer", "inner")),
        P(),
        P(),
    )
    return jax.shard_map(
        body,
        mesh=mesh,
        in_specs=placed,
        out_specs=(P(), P(), P(("outer", "inner"), None), P(("outer", "inner"), None)),
        check_vma=False,
    )
```
